32 devices in a mesh: rep: 4 (over x, core), dp: 4 (over z), expert: 2 (over y).
Axes of the slice: x: 2, y: 2, z: 4, core: 2. Of those that a mesh axis runs over, the one named last changes fastest.
Arguments:
- tokens: bfloat16 [8192, 768], P(('rep', 'dp', 'expert')), may hold values from -6 to 6
- doc_ids: int32 [8192], P(('rep', 'dp', 'expert')), may hold values from 0 to 255, as said below
- routes: int32 [8192, 1], P(('rep', 'dp', 'expert')), may hold values from 0 to 1; in each aligned block of 256 rows (0 to 255, 256 to 511, ...) at most 256 rows name the same one
- cotangent: bfloat16 [8192, 768], P(('rep', 'dp', 'expert')), may hold values from -6 to 6
- attn_gain: bfloat16 [768], P(('dp', 'expert')), may hold values from 0.5 to 1.5
- w_query: bfloat16 [768, 768], P(('dp', 'expert')), may hold values from -0.02734375 to 0.02734375
- w_key: bfloat16 [768, 768], P(('dp', 'expert')), may hold values from -0.02734375 to 0.02734375
- w_value: bfloat16 [768, 768], P(('dp', 'expert')), may hold values from -0.21875 to 0.21875
- w_output: bfloat16 [768, 768], P(('dp', 'expert')), may hold values from -0.75 to 0.75
- rel_table: float32 [32, 12], replicated, may hold values from -4 to 4
- ffn_gain: bfloat16 [768], P(('dp', 'expert')), may hold values from 0.5 to 1.5
- w_router: bfloat16 [768, 2], P(('dp', 'expert')), may hold values from -0.21875 to 0.21875
- w_in: bfloat16 [2, 768, 3072], P('expert'), may hold values from -0.21875 to 0.21875
- w_out: bfloat16 [2, 3072, 768], P('expert'), may hold values from -0.21875 to 0.21875
Outputs:
- mixed: bfloat16 [8192, 768], P(('rep', 'dp', 'expert'))
- grad_tokens: float32 [8192, 768], P(('rep', 'dp', 'expert'))
- grad_attn_gain: float32 [768], P(('dp', 'expert'))
- grad_query: float32 [768, 768], P(('dp', 'expert'))
- grad_key: float32 [768, 768], P(('dp', 'expert'))
- grad_value: float32 [768, 768], P(('dp', 'expert'))
- grad_output: float32 [768, 768], P(('dp', 'expert'))
- grad_rel_table: float32 [32, 12], replicated
- grad_ffn_gain: float32 [768], P(('dp', 'expert'))
- grad_router: float32 [768, 2], P(('dp', 'expert'))
- grad_w_in: float32 [2, 768, 3072], P('expert', 'dp')
- grad_w_out: float32 [2, 3072, 768], P('expert', 'dp')
The draws below stay inside these ranges and needn't reach their ends.
Inputs may be any that keep to these rules, and one draw needn't show every extreme that they name: `doc_ids`: along each device's 256 tokens the ids start at 0 and rise by 0 or 1 from token to token; equal ids mark one document. On some device all 256 tokens form one document, and on another every token is a document of its own. `routes`: among the 256 tokens of one device at most 256 name the same expert, and in every draw some expert is named by exactly 256 of them.
All inputs are finite; a program needn't handle non-finite values.
Results may differ from the reference program's by a relative error of at most 0.012.
Values may be sent and summed in bfloat16 or wider, within the bound.
No kernel may reach another device: no remote copies, remote signals or barrier semaphores. Data moves between devices by JAX's collectives and lax.ppermute only.
A program may use at most 128 MiB of HBM per device.

```python
import math
from functools import partial
import jax
import jax.numpy as jnp
import numpy as np
from jax import lax

D = 768
HEADS = 12
HEAD_DIM = 64
FF = 3072
BUCKETS = 32
TOK_DEV = 256
TOKENS = 8192
EXPERTS = 2
CAP = 256


def draw_doc_ids(key, part):
    key = jax.random.fold_in(key, 7)
    cut_key, rate_key, row_key, single_key = jax.random.split(key, 4)
    device_rows = TOKENS // TOK_DEV
    rate_table = jnp.array([4, 32, 256], dtype=jnp.int32)
    rate_levels = jax.random.randint(rate_key, (device_rows, 1), 0, 3)
    row_rates = rate_table[rate_levels]
    cut_flags = jax.random.randint(cut_key, (device_rows, TOK_DEV), 0, 1024) < row_rates
    whole_row = jax.random.randint(row_key, (), 0, device_rows)
    single_row = (whole_row + jax.random.randint(single_key, (), 1, device_rows)) % device_rows
    row_ids = jnp.arange(device_rows, dtype=jnp.int32)[:, None]
    col_ids = jnp.arange(TOK_DEV, dtype=jnp.int32)[None, :]
    cut_flags = (cut_flags | (row_ids == single_row)) & (col_ids > 0) & (row_ids != whole_row)
    return jnp.cumsum(cut_flags.astype(jnp.int32), axis=1).reshape(TOKENS).astype(jnp.int32)


def shard_levels(own_key, extent, pieces, smallest, top_value):
    def one(dim, shards_of):
        steps = jax.random.uniform(jax.random.fold_in(jax.random.fold_in(own_key, 6), dim), (shards_of,), jnp.float32, smallest / len(pieces), top_value / len(pieces))
        return jnp.repeat(jnp.exp(steps), extent[dim] // shards_of).reshape((-1,) + (1,) * (len(extent) - dim - 1))

    factor_of = one(*pieces[0])
    for cut in pieces[1:]:
        factor_of = factor_of * one(*cut)
    return factor_of


def routed_block(stream_key, own, number, rows, count, top, limit, lean):
    order = jax.random.permutation(stream_key, count)
    heavy_load, common = shares(count, rows * top, limit, lean, True), shares(count, rows * top, limit, lean, False)
    places = jnp.arange(count)

    def named(sizes, turn):
        used = int((sizes > 0).sum())
        fixed = max(1, used // 4)
        moved = fixed + (places - fixed + turn * (used - fixed)) % max(1, count - fixed)
        return jnp.zeros((count,), jnp.int32).at[order[jnp.where(places < fixed, places, moved)]].set(jnp.asarray(sizes, jnp.int32))

    sizes = jnp.where(number % 4 == 0, named(heavy_load, number // 4), named(common, number - number // 4 - 1))
    mixed = jax.random.permutation(jax.random.fold_in(own, 3), count)
    donor, receiver = mixed[0:count // 2 * 2:2], mixed[1:count // 2 * 2:2]
    margin = jnp.minimum(sizes[donor] - 1, limit - sizes[receiver]) // 2
    margin = jnp.where((donor == order[0]) | (receiver == order[0]) | (sizes[receiver] == 0), 0, jnp.maximum(margin, 0))
    moved = jax.random.randint(jax.random.fold_in(own, 4), (count // 2,), 0, 1 << 20) % (margin + 1)
    sizes = sizes.at[donor].add(-moved).at[receiver].add(moved)
    members = jnp.searchsorted(jnp.cumsum(sizes), jnp.arange(rows * top), side="right").astype(jnp.int32)
    table = members.reshape(top, rows).T
    table = table[jax.random.permutation(jax.random.fold_in(own, 1), rows)]
    turn = jax.random.randint(jax.random.fold_in(own, 2), (rows, 1), 0, top)
    return jnp.take_along_axis(table, (jnp.arange(top)[None, :] + turn) % top, axis=1)


def shares(count, total, most, skew, full):
    weights = [(1 << 20) // math.isqrt(rank ** skew) + 1 for rank in range(1, count + 1)]
    largest = most if full else min(most, max(-(-total // count), total * weights[0] // sum(weights)))
    least = 1 if total - largest >= count - 1 else 0
    counts, spare = [largest] + [least] * (count - 1), total - largest - least * (count - 1)
    while spare > 0:
        movable = [i for i in range(1, count) if counts[i] < largest] or [i for i in range(1, count) if counts[i] < most]
        whole, left = sum([weights[i] for i in movable]), spare
        for i in movable:
            more = min(most - counts[i], max(1, left * weights[i] // whole), spare)
            counts[i] = counts[i] + more
            spare = spare - more
    return np.array(counts)


def noise(rng, shape, width, limit, shards=(), kind=jnp.bfloat16):
    drawn = jax.random.normal(rng, shape, jnp.float32) * width
    if len(shards) > 0:
        drawn = shard_levels(rng, shape, shards, -0.22, 0.18) * drawn
    return jnp.clip(drawn, min=-limit, max=limit).astype(kind)


def setup_inputs(seed: int = 0) -> dict:
    streams_of = jax.random.split(jax.random.key(seed), 15)
    tokens = noise(streams_of[0], (TOKENS, D), 1.0, 6.0, ((0, 32),))
    doc_ids = draw_doc_ids(jax.random.fold_in(streams_of[14], 71), 0)
    routes_keys = jax.random.split(jax.random.fold_in(streams_of[2], 1), TOKENS // TOK_DEV)
    routes_turns = jax.random.permutation(jax.random.fold_in(streams_of[2], 3), TOKENS // TOK_DEV)
    routes = jax.vmap(lambda own, number: routed_block(jax.random.fold_in(streams_of[2], 2), own, number, TOK_DEV, EXPERTS, 1, CAP, 2))(routes_keys, routes_turns).reshape((TOKENS, 1))
    cotangent = noise(streams_of[3], (TOKENS, D), 1.0, 6.0, ((0, 32),))
    attn_gain = jnp.clip(1.0 + 0.1 * jax.random.normal(streams_of[4], (D,), jnp.float32), 0.5, 1.5).astype(jnp.bfloat16)
    w_query = noise(streams_of[5], (D, D), (D * HEAD_DIM) ** -0.5, 0.02734375, ((0, 8),))
    w_key = noise(streams_of[6], (D, D), (D * HEAD_DIM) ** -0.5, 0.02734375, ((0, 8),))
    w_value = noise(streams_of[7], (D, D), D ** -0.5, 0.21875, ((0, 8),))
    w_output = noise(streams_of[8], (D, D), HEAD_DIM ** -0.5, 0.75, ((0, 8),))
    rel_table = noise(streams_of[9], (BUCKETS, HEADS), 1.0, 4.0, (), jnp.float32)
    ffn_gain = jnp.clip(1.0 + 0.1 * jax.random.normal(streams_of[10], (D,), jnp.float32), 0.5, 1.5).astype(jnp.bfloat16)
    w_router = noise(streams_of[11], (D, EXPERTS), D ** -0.5, 0.21875, ((0, 8),))
    w_in = noise(streams_of[12], (EXPERTS, D, FF), D ** -0.5, 0.21875, ((0, 2),))
    w_out = noise(streams_of[13], (EXPERTS, FF, D), (max(1, FF // (EXPERTS * EXPERTS))) ** -0.5, 0.21875, ((0, 2),))
    return {"tokens": tokens, "doc_ids": doc_ids, "routes": routes, "cotangent": cotangent, "attn_gain": attn_gain, "w_query": w_query, "w_key": w_key, "w_value": w_value, "w_output": w_output, "rel_table": rel_table, "ffn_gain": ffn_gain, "w_router": w_router, "w_in": w_in, "w_out": w_out}


EPSILON = 1e-06
BUCKET_BOUNDS = (12, 16, 23, 32, 46, 64, 91)

@jax.custom_vjp
def low(v):
    return lax.optimization_barrier(v.astype(jnp.bfloat16)).astype(jnp.float32)

@jax.custom_vjp
def low_back(v):
    return v

def low_keep(v):
    return (low(v), None)

def low_pass(kept, grad):
    return (grad,)

def back_keep(v):
    return (v, None)

def back_low(kept, grad):
    return (low(grad),)
low.defvjp(low_keep, low_pass)
low_back.defvjp(back_keep, back_low)

def bucket_of(offsets):
    distance = jnp.abs(offsets)
    levels = jnp.minimum(distance, 8)
    for threshold in BUCKET_BOUNDS:
        levels = levels + (distance >= threshold).astype(jnp.int32)
    return levels + 16 * (offsets > 0).astype(jnp.int32)

def rms_norm(values, gain_values):
    factor = lax.rsqrt(lax.optimization_barrier(jnp.mean(values * values, axis=-1, keepdims=True)) + EPSILON)
    return values * factor * gain_values

def device_attention(arrays, bias_table):
    queries, key_heads, value_heads, doc_block = arrays
    tok_rows = queries.shape[0]
    places = jnp.arange(tok_rows, dtype=jnp.int32)
    buckets = bucket_of(places[None, :] - places[:, None])
    bias = jnp.transpose(bias_table[buckets], (2, 0, 1))
    scores = jnp.einsum('qhd,khd->hqk', queries, key_heads, precision=lax.Precision.HIGHEST) + bias
    scores = low_back(scores)
    same_doc = doc_block[:, None] == doc_block[None, :]
    attn_probs = low(jax.nn.softmax(jnp.where(same_doc[None], scores, -1e+30), axis=-1))
    return jnp.einsum('hqk,khd->qhd', attn_probs, value_heads, precision=lax.Precision.HIGHEST)

def block_forward(doc_ids, routes, inputs, attn_gain, w_query, w_key, w_value, w_output, rel_table, ffn_gain, w_router, w_in, w_out):
    total_rows, model_width = inputs.shape
    head_count = rel_table.shape[1]
    head_size = model_width // head_count
    groups = total_rows // TOK_DEV
    normed_one = low(rms_norm(inputs, attn_gain))

    def project(matrix):
        made = low(low_back(jnp.dot(normed_one, matrix, precision=lax.Precision.HIGHEST)))
        return made.reshape(groups, TOK_DEV, head_count, head_size)
    queries = project(w_query)
    key_heads = project(w_key)
    value_heads = project(w_value)
    attended = lax.map(jax.checkpoint(partial(device_attention, bias_table=rel_table)), (queries, key_heads, value_heads, doc_ids.reshape(groups, TOK_DEV)))
    attended = low(low_back(attended.reshape(total_rows, model_width)))
    residual = inputs + low_back(jnp.dot(attended, w_output, precision=lax.Precision.HIGHEST))
    normed_two = low(rms_norm(residual, ffn_gain))
    logits = low_back(jnp.dot(normed_two, w_router, precision=lax.Precision.HIGHEST))
    router_probs = jax.nn.softmax(logits, axis=-1)
    gate_values = jnp.take_along_axis(router_probs, routes, axis=1)[:, 0]
    expert_in = low_back(normed_two)
    route_ids = routes[:, 0]
    chosen = (route_ids.reshape(groups, TOK_DEV)[:, :, None] == jnp.arange(EXPERTS, dtype=jnp.int32)[None, None, :]).astype(jnp.int32)
    slot_rank = (lax.optimization_barrier(jnp.sum(jnp.cumsum(chosen, axis=1) * chosen, axis=-1)) - 1).reshape(total_rows).astype(jnp.int32)
    owners = jnp.repeat(jnp.arange(groups, dtype=jnp.int32), TOK_DEV)
    slots_in = jnp.zeros((EXPERTS, groups, CAP, model_width), jnp.float32).at[route_ids, owners, slot_rank].set(expert_in)

    def run_expert(arrays):
        row_block, first_weight, second_weight = arrays
        pre_act = low_back(jnp.dot(row_block.reshape(groups * CAP, model_width), first_weight, precision=lax.Precision.HIGHEST))
        hidden = low(jax.nn.gelu(pre_act, approximate=False))
        made = low(low_back(jnp.dot(hidden, second_weight, precision=lax.Precision.HIGHEST)))
        return made.reshape(groups, CAP, model_width)
    produced = lax.map(jax.checkpoint(run_expert), (slots_in, w_in, w_out))
    expert_rows = produced[route_ids, owners, slot_rank]
    return residual + gate_values[:, None] * expert_rows

def reference(tokens, doc_ids, routes, cotangent, attn_gain, w_query, w_key, w_value, w_output, rel_table, ffn_gain, w_router, w_in, w_out):
    floats = [array_in.astype(jnp.float32) for array_in in (tokens, attn_gain, w_query, w_key, w_value, w_output, rel_table, ffn_gain, w_router, w_in, w_out)]
    result, pullback = jax.vjp(partial(block_forward, doc_ids, routes), *floats)
    gradients = pullback(cotangent.astype(jnp.float32))
    return (result.astype(jnp.bfloat16), gradients[0], gradients[1], gradients[2], gradients[3], gradients[4], gradients[5], gradients[6], gradients[7], gradients[8], gradients[9], gradients[10])
```

```python
import jax
import jax.numpy as jnp
from jax import lax
from jax.sharding import PartitionSpec as P

EPSILON = 1e-06
BUCKET_BOUNDS = (12, 16, 23, 32, 46, 64, 91)
INV_ROOT_TWO = 0.7071067811865476
INV_ROOT_TWO_PI = 0.3989422804014327
BF16 = jnp.bfloat16
F32 = jnp.float32


def bucket_of(offsets):
    distance = jnp.abs(offsets)
    levels = jnp.minimum(distance, 8)
    for threshold in BUCKET_BOUNDS:
        levels = levels + (distance >= threshold).astype(jnp.int32)
    return levels + 16 * (offsets > 0).astype(jnp.int32)


def bucket_onehot(tok_rows, bucket_count):
    window = 2 * tok_rows
    places = jnp.arange(window, dtype=jnp.int32)
    offsets = jnp.where(places < tok_rows, places, places - window)
    return (
        bucket_of(offsets)[:, None] == jnp.arange(bucket_count, dtype=jnp.int32)[None, :]
    ).astype(F32)


def skew_bias(diag_values, tok_rows):
    head_count, window = diag_values.shape
    repeated = jnp.broadcast_to(diag_values[:, None, :], (head_count, tok_rows, window))
    flattened = repeated.reshape(head_count, tok_rows * window)[:, : tok_rows * (window - 1)]
    return flattened.reshape(head_count, tok_rows, window - 1)[:, :, :tok_rows]


def unskew_sum(grad_block, tok_rows):
    head_count = grad_block.shape[0]
    window = 2 * tok_rows
    padded = jnp.pad(grad_block, ((0, 0), (0, 0), (0, window - 1 - tok_rows)))
    flattened = jnp.pad(padded.reshape(head_count, tok_rows * (window - 1)), ((0, 0), (0, tok_rows)))
    return jnp.sum(flattened.reshape(head_count, tok_rows, window), axis=1)


def rep_swap(values, bit):
    count = lax.axis_size("rep")
    return lax.ppermute(values, "rep", [(i, i ^ bit) for i in range(count)])


def shift(values, axis, step):
    count = lax.axis_size(axis)
    return lax.ppermute(values, axis, [(i, (i + step) % count) for i in range(count)])


def pick(values, index, axis):
    return lax.dynamic_index_in_dim(values, index, axis, keepdims=False)


def gather_axis(values, axis):
    count = lax.axis_size(axis)
    if count > 4:
        return lax.all_gather(values, axis, axis=0)
    place = lax.axis_index(axis)
    out = jnp.zeros((count,) + values.shape, values.dtype)
    out = lax.dynamic_update_index_in_dim(out, values, place, 0)
    for step in range(1, count):
        got = shift(values, axis, step)
        out = lax.dynamic_update_index_in_dim(out, got, (place - step) % count, 0)
    return out


def pair_stack(values, bit, low):
    got = rep_swap(values, bit)
    return jnp.where(low == 0, jnp.stack([values, got]), jnp.stack([got, values]))


def gather_rep(values, high, low):
    both = pair_stack(values, 2, high)
    four = pair_stack(both, 1, low)
    return jnp.swapaxes(four, 0, 1).reshape((4,) + values.shape)


def add_pair(one, two):
    return (one.astype(F32) + two.astype(F32)).astype(BF16)


def sum_axis(values, axis):
    count = lax.axis_size(axis)
    if count > 4:
        return lax.psum_scatter(values.astype(F32), axis, scatter_dimension=0, tiled=False).astype(BF16)
    place = lax.axis_index(axis)
    total = pick(values, place, 0).astype(F32)
    for step in range(1, count):
        total = total + shift(pick(values, (place + step) % count, 0), axis, step).astype(F32)
    return total.astype(BF16)


def halve(values, bit, low, axis):
    got = rep_swap(pick(values, 1 - low, axis), bit)
    return add_pair(pick(values, low, axis), got)


def local(
    tokens,
    doc_ids,
    routes,
    cotangent,
    attn_gain,
    w_query,
    w_key,
    w_value,
    w_output,
    rel_table,
    ffn_gain,
    w_router,
    w_in,
    w_out,
):
    tok_rows, model_width = tokens.shape
    head_count = rel_table.shape[1]
    head_size = model_width // head_count
    experts = w_router.shape[1]
    dp_count = lax.axis_size("dp")
    expert_axis = lax.axis_size("expert")
    capacity = 2 * tok_rows // expert_axis
    rep = lax.axis_index("rep")
    high, low = rep // 2, rep % 2
    me = lax.axis_index("expert")
    shard_rows = w_query.shape[0]

    small = jnp.concatenate([attn_gain[:, None], ffn_gain[:, None], w_router], axis=1)
    small = gather_axis(gather_axis(small, "dp"), "expert")
    small = jnp.swapaxes(small, 0, 1).reshape(model_width, 2 + experts)
    gain_one = small[:, 0].astype(F32)
    gain_two = small[:, 1].astype(F32)
    router_full = small[:, 2:]

    def gather_weights(matrices):
        wide = jnp.concatenate(matrices, axis=1)
        width = wide.shape[1] // 4
        mine = lax.dynamic_slice_in_dim(wide, rep * width, width, 1)
        mine = gather_axis(gather_axis(mine, "dp"), "expert")
        mine = jnp.swapaxes(mine, 0, 1).reshape(model_width, width)
        parts = gather_rep(mine, high, low)
        return parts

    qk_parts = gather_weights((w_query, w_key))
    vo_parts = gather_weights((w_value, w_output))
    query_full = jnp.concatenate([qk_parts[0], qk_parts[1]], axis=1)
    key_full = jnp.concatenate([qk_parts[2], qk_parts[3]], axis=1)
    value_full = jnp.concatenate([vo_parts[0], vo_parts[1]], axis=1)
    output_full = jnp.concatenate([vo_parts[2], vo_parts[3]], axis=1)

    route_ids = routes[:, 0]
    direct = expert_axis == 2 and capacity == tok_rows
    if direct:

        def send(values):
            return jnp.concatenate([values, shift(values, "expert", 1)], axis=0)

        def back(rows):
            other = shift(rows[tok_rows:], "expert", 1)
            return jnp.where((route_ids == me)[:, None], rows[:tok_rows], other)

        valid = (send(routes)[:, 0] == me).astype(F32)
    else:
        chosen = (route_ids[:, None] == jnp.arange(experts, dtype=jnp.int32)[None, :]).astype(jnp.int32)
        slot_rank = jnp.sum(jnp.cumsum(chosen, axis=0) * chosen, axis=-1) - 1
        slot_index = route_ids * capacity + slot_rank
        place_of = (
            jnp.arange(experts * capacity, dtype=jnp.int32)[:, None] == slot_index[None, :]
        ).astype(BF16)

        def send(values):
            slots = jnp.dot(place_of, values, preferred_element_type=F32).astype(BF16)
            return lax.all_to_all(slots, "expert", split_axis=0, concat_axis=0, tiled=True)

        def back(rows):
            slots = lax.all_to_all(rows, "expert", split_axis=0, concat_axis=0, tiled=True)
            return jnp.dot(place_of.T, slots, preferred_element_type=F32).astype(BF16)

        valid = send(jnp.ones((tok_rows, 1), BF16))[:, 0].astype(F32)

    first_weight = w_in[0]
    second_weight = w_out[0]
    slot_cot = send(cotangent)
    slot_back = jnp.einsum("td,fd->tf", slot_cot, second_weight, preferred_element_type=F32).astype(BF16)

    onehot = bucket_onehot(tok_rows, rel_table.shape[0])
    diag_values = jnp.dot(onehot, rel_table, precision=lax.Precision.HIGHEST).T
    bias = skew_bias(diag_values, tok_rows)
    same_doc = doc_ids[:, None] == doc_ids[None, :]
    bias = jnp.where(same_doc[None], bias, -1e30)

    inputs = tokens.astype(F32)
    factor_one = lax.rsqrt(jnp.mean(inputs * inputs, axis=-1, keepdims=True) + EPSILON)
    normed_one = (inputs * factor_one * gain_one).astype(BF16)

    def heads_of(matrix):
        made = jnp.dot(normed_one, matrix, preferred_element_type=F32).astype(BF16)
        return made.reshape(tok_rows, head_count, head_size)

    queries = heads_of(query_full)
    key_heads = heads_of(key_full)
    value_heads = heads_of(value_full)
    scores = jnp.einsum("qhd,khd->hqk", queries, key_heads, preferred_element_type=F32) + bias
    scores = jnp.where(same_doc[None], scores, -1e30)
    row_max = jnp.max(scores, axis=-1, keepdims=True)
    exponent = jnp.exp(scores - row_max)
    attn_probs = exponent / jnp.sum(exponent, axis=-1, keepdims=True)
    probs_low = attn_probs.astype(BF16)
    attended = jnp.einsum("hqk,khd->qhd", probs_low, value_heads, preferred_element_type=F32)
    attended = attended.astype(BF16).reshape(tok_rows, model_width)
    residual = inputs + jnp.dot(attended, output_full, preferred_element_type=F32)
    factor_two = lax.rsqrt(jnp.mean(residual * residual, axis=-1, keepdims=True) + EPSILON)
    normed_two = (residual * factor_two * gain_two).astype(BF16)
    probs_two = jax.nn.softmax(jnp.dot(normed_two, router_full, preferred_element_type=F32), axis=-1)
    own_gate = jnp.sum(
        probs_two * (route_ids[:, None] == jnp.arange(experts, dtype=jnp.int32)[None, :]), axis=-1
    )

    rows_in = send(normed_two)
    slot_probs = jax.nn.softmax(jnp.dot(rows_in, router_full, preferred_element_type=F32), axis=-1)
    is_me = (jnp.arange(experts, dtype=jnp.int32) == me).astype(F32)
    slot_gate = jnp.sum(slot_probs * is_me[None, :], axis=-1) * valid
    pre_act = jnp.dot(rows_in, first_weight, preferred_element_type=F32)
    cdf = 0.5 * (1.0 + lax.erf(pre_act * INV_ROOT_TWO))
    hidden = (pre_act * cdf).astype(BF16)
    slope = cdf + pre_act * jnp.exp(-0.5 * pre_act * pre_act) * INV_ROOT_TWO_PI
    grad_pre = (slot_back.astype(F32) * slot_gate[:, None] * slope).astype(BF16)
    produced = jnp.dot(hidden, second_weight, preferred_element_type=F32).astype(BF16)
    slot_cot_wide = slot_cot.astype(F32)
    grad_gate = jnp.sum(slot_cot_wide * produced.astype(F32), axis=-1)
    grad_logits = ((grad_gate * slot_gate)[:, None] * (is_me[None, :] - slot_probs)).astype(BF16)
    grad_rows = jnp.einsum("tf,df->td", grad_pre, first_weight, preferred_element_type=F32)
    grad_rows = grad_rows + jnp.einsum("te,de->td", grad_logits, router_full, preferred_element_type=F32)
    grad_normed_two = back(grad_rows.astype(BF16)).astype(F32)
    expert_rows = back(produced).astype(F32)
    mixed = (residual + own_gate[:, None] * expert_rows).astype(BF16)
    grad_expert = (slot_cot_wide * slot_gate[:, None]).astype(BF16)
    grad_router = jnp.einsum("td,te->de", rows_in, grad_logits, preferred_element_type=F32)
    grad_second = jnp.einsum("tf,td->fd", hidden, grad_expert, preferred_element_type=F32).astype(BF16)
    grad_first = jnp.einsum("td,tf->df", rows_in, grad_pre, preferred_element_type=F32).astype(BF16)

    def split_expert(matrix):
        rows, columns = matrix.shape
        return matrix.reshape(dp_count, 2, 2, rows // (4 * dp_count), columns)

    def finish(part):
        four = gather_rep(part, high, low)
        return four.reshape(1, -1, part.shape[-1]).astype(F32)

    part_second = halve(split_expert(grad_second), 1, low, 2)
    part_second = sum_axis(part_second, "dp")
    part_second = halve(part_second, 2, high, 0)
    grad_w_out = finish(part_second)
    part_first = halve(split_expert(grad_first), 1, low, 2)
    part_first = halve(part_first, 2, high, 1)
    part_first = sum_axis(part_first, "dp")
    grad_w_in = finish(part_first)

    def norm_back(grad_out, values, factor, gain):
        scaled = grad_out * gain
        inner = jnp.mean(scaled * values, axis=-1, keepdims=True)
        grad_gain = jnp.sum(grad_out * values * factor, axis=0)
        return factor * scaled - values * (factor * factor * factor) * inner, grad_gain

    grad_mixed = cotangent.astype(F32)
    grad_residual, grad_ffn_gain = norm_back(grad_normed_two, residual, factor_two, gain_two)
    grad_residual = grad_mixed + grad_residual
    grad_attn = grad_residual.astype(BF16)
    grad_output = jnp.einsum("tc,td->cd", attended, grad_attn, preferred_element_type=F32).astype(BF16)
    grad_attended = jnp.einsum("td,cd->tc", grad_attn, output_full, preferred_element_type=F32).astype(BF16)
    grad_attended = grad_attended.reshape(tok_rows, head_count, head_size)
    grad_probs = jnp.einsum("qhd,khd->hqk", grad_attended, value_heads, preferred_element_type=F32)
    grad_values = jnp.einsum("hqk,qhd->khd", probs_low, grad_attended, preferred_element_type=F32)
    inner = jnp.sum(attn_probs * grad_probs, axis=-1, keepdims=True)
    grad_scores = (attn_probs * (grad_probs - inner)).astype(BF16)
    grad_queries = jnp.einsum("hqk,khd->qhd", grad_scores, key_heads, preferred_element_type=F32)
    grad_keys = jnp.einsum("hqk,qhd->khd", grad_scores, queries, preferred_element_type=F32)
    diag_grads = unskew_sum(grad_scores.astype(F32), tok_rows)
    grad_table = jnp.dot(onehot.T, diag_grads.T, precision=lax.Precision.HIGHEST)
    grad_queries = grad_queries.astype(BF16).reshape(tok_rows, model_width)
    grad_keys = grad_keys.astype(BF16).reshape(tok_rows, model_width)
    grad_values = grad_values.astype(BF16).reshape(tok_rows, model_width)

    def weight_grad(grads):
        return jnp.einsum("td,tc->dc", normed_one, grads, preferred_element_type=F32).astype(BF16)

    stacked = jnp.stack(
        [weight_grad(grad_queries), weight_grad(grad_keys), weight_grad(grad_values), grad_output]
    )
    stacked = stacked.reshape(2, 2, dp_count, expert_axis, shard_rows, model_width)
    part = halve(stacked, 1, low, 1)
    part = sum_axis(jnp.moveaxis(part, 2, 0), "expert")
    part = halve(part, 2, high, 0)
    part = sum_axis(part, "dp")
    owned = gather_rep(part, high, low).astype(F32)

    grad_normed_one = jnp.einsum("tc,dc->td", grad_queries, query_full, preferred_element_type=F32)
    grad_normed_one = grad_normed_one + jnp.einsum(
        "tc,dc->td", grad_keys, key_full, preferred_element_type=F32
    )
    grad_normed_one = grad_normed_one + jnp.einsum(
        "tc,dc->td", grad_values, value_full, preferred_element_type=F32
    )
    grad_inputs, grad_attn_gain = norm_back(grad_normed_one, inputs, factor_one, gain_one)
    grad_tokens = grad_residual + grad_inputs

    packed = jnp.concatenate(
        [grad_attn_gain, grad_ffn_gain, grad_router.T.reshape(-1), grad_table.reshape(-1)]
    )
    packed = lax.psum(packed, ("rep", "dp", "expert"))
    row_start = (lax.axis_index("dp") * expert_axis + me) * shard_rows
    wide = packed[: (2 + experts) * model_width].reshape(2 + experts, model_width)
    wide = lax.dynamic_slice_in_dim(wide, row_start, shard_rows, 1)
    table_total = packed[(2 + experts) * model_width :].reshape(rel_table.shape)
    return (
        mixed,
        grad_tokens,
        wide[0],
        owned[0],
        owned[1],
        owned[2],
        owned[3],
        table_total,
        wide[1],
        wide[2:].T,
        grad_w_in,
        grad_w_out,
    )


def solution(mesh):
    rows = P(("rep", "dp", "expert"), None)
    split = P(("dp", "expert"), None)
    vector = P(("dp", "expert"))
    return jax.shard_map(
        local,
        mesh=mesh,
        in_specs=(
            rows,
            P(("rep", "dp", "expert")),
            rows,
            rows,
            vector,
            split,
            split,
            split,
            split,
            P(),
            vector,
            split,
            P("expert", None, None),
            P("expert", None, None),
        ),
        out_specs=(
            rows,
            rows,
            vector,
            split,
            split,
            split,
            split,
            P(),
            vector,
            split,
            P("expert", "dp", None),
            P("expert", "dp", None),
        ),
        check_vma=False,
    )
```

```python
import functools

import jax
import jax.numpy as jnp
from jax import lax
from jax.experimental import pallas as pl
from jax.experimental.pallas import tpu as pltpu
from jax.sharding import PartitionSpec as P

EPSILON = 1e-06
BUCKET_BOUNDS = (12, 16, 23, 32, 46, 64, 91)
INV_ROOT_TWO = 0.7071067811865476
INV_ROOT_TWO_PI = 0.3989422804014327
BF16 = jnp.bfloat16
F32 = jnp.float32


def bucket_of(offsets):
    distance = jnp.abs(offsets)
    levels = jnp.minimum(distance, 8)
    for threshold in BUCKET_BOUNDS:
        levels = levels + (distance >= threshold).astype(jnp.int32)
    return levels + 16 * (offsets > 0).astype(jnp.int32)


def bucket_onehot(tok_rows, bucket_count):
    window = 2 * tok_rows
    places = jnp.arange(window, dtype=jnp.int32)
    offsets = jnp.where(places < tok_rows, places, places - window)
    return (
        bucket_of(offsets)[:, None] == jnp.arange(bucket_count, dtype=jnp.int32)[None, :]
    ).astype(F32)


def rep_swap(values, bit):
    count = lax.axis_size("rep")
    return lax.ppermute(values, "rep", [(i, i ^ bit) for i in range(count)])


def shift(values, axis, step):
    count = lax.axis_size(axis)
    return lax.ppermute(values, axis, [(i, (i + step) % count) for i in range(count)])


def pick(values, index, axis):
    return lax.dynamic_index_in_dim(values, index, axis, keepdims=False)


def add_pair(one, two):
    return (one.astype(F32) + two.astype(F32)).astype(BF16)


def sum_over(values, axis, dimension):
    total = lax.psum_scatter(values.astype(F32), axis, scatter_dimension=dimension, tiled=False)
    return total.astype(BF16)


VMEM_BYTES = 32 * 1024 * 1024
BIG = 40
NT = (((1,), (1,)), ((), ()))
TN = (((0,), (0,)), ((), ()))


def mm(one, two):
    return jnp.dot(one, two, preferred_element_type=F32)


def mm_nt(one, two):
    return lax.dot_general(one, two, NT, preferred_element_type=F32)


def mm_tn(one, two):
    return lax.dot_general(one, two, TN, preferred_element_type=F32)


def estimate(us):
    return pl.CostEstimate(flops=us * 10**9 + 1, bytes_accessed=us * 10**6 + 1, transcendentals=0)


def whole_call(kernel, outs, scalars, arrays, scratch=(), us=2):
    vmem = pl.BlockSpec(memory_space=pltpu.VMEM)
    return pl.pallas_call(
        kernel,
        out_shape=[jax.ShapeDtypeStruct(s, d) for s, d in outs],
        in_specs=[pl.BlockSpec(memory_space=pltpu.SMEM)] * len(scalars) + [vmem] * len(arrays),
        out_specs=[vmem] * len(outs),
        scratch_shapes=list(scratch),
        cost_estimate=estimate(us),
        compiler_params=pltpu.CompilerParams(vmem_limit_bytes=VMEM_BYTES),
    )(*scalars, *arrays)


def bias_kernel(diag_ref, row_ref, col_ref, bias_ref):
    heads, tok, _ = bias_ref.shape
    window = diag_ref.shape[1]
    same = row_ref[...] == col_ref[...]
    for head in range(heads):
        wide = jnp.broadcast_to(diag_ref[head : head + 1, :], (tok, window))
        rolled = pltpu.roll(wide, 0, 1, stride=1, stride_axis=0)
        bias_ref[head] = jnp.where(same, rolled[:, :tok], -1e30)


def choose(place_ref, target, pieces):
    at = jnp.bitwise_xor(2 * place_ref[0] + place_ref[1], target)
    near = jnp.where(at % 2 == 0, pieces[0][...], pieces[1][...])
    far = jnp.where(at % 2 == 0, pieces[2][...], pieces[3][...])
    return jnp.where(at < 2, near, far)


def weight_halves(place_ref, index, pieces):
    return choose(place_ref, 2 * index, pieces), choose(place_ref, 2 * index + 1, pieces)


def project(values, halves):
    return jnp.concatenate([mm(values, halves[0]), mm(values, halves[1])], axis=1)


def project_back(turned, halves):
    half = turned.shape[0] // 2
    return mm(halves[0], turned[:half]) + mm(halves[1], turned[half:])


def low_lanes(tok, head_size):
    return lax.broadcasted_iota(jnp.int32, (tok, 2 * head_size), 1) < head_size


def scores_kernel(place_ref, tokens_ref, gain_ref, *refs):
    pieces = refs[:4]
    bias_ref, normed_ref, q_ref, k_ref, probs_ref = refs[4:]
    heads, tok, _ = bias_ref.shape
    size = tokens_ref.shape[1] // heads
    values = tokens_ref[...].astype(F32)
    factor = lax.rsqrt(jnp.mean(values * values, axis=-1, keepdims=True) + EPSILON)
    normed = (values * factor * gain_ref[...]).astype(BF16)
    normed_ref[...] = normed
    q_ref[...] = project(normed, weight_halves(place_ref, 0, pieces)).astype(BF16)
    k_ref[...] = project(normed, weight_halves(place_ref, 1, pieces)).astype(BF16)
    first = low_lanes(tok, size)
    for pair in range(heads // 2):
        lanes = slice(pair * 2 * size, (pair + 1) * 2 * size)
        queries, keys = q_ref[:, lanes], k_ref[:, lanes]
        for part in range(2):
            head = 2 * pair + part
            picked = jnp.where(first if part == 0 else ~first, queries, jnp.zeros_like(queries))
            scores = mm_nt(picked, keys) + bias_ref[head]
            exponent = jnp.exp(scores - jnp.max(scores, axis=-1, keepdims=True))
            probs = exponent / jnp.sum(exponent, axis=-1, keepdims=True)
            probs_ref[head] = probs.astype(BF16)


def attend_kernel(
    experts,
    place_ref,
    tokens_ref,
    normed_ref,
    gain_ref,
    router_ref,
    routes_ref,
    *refs,
):
    pieces = refs[:4]
    probs_ref, v_ref, attended_ref, residual_ref, normed_two_ref, gate_ref = refs[4:]
    heads, tok, _ = probs_ref.shape
    size = tokens_ref.shape[1] // heads
    v_ref[...] = project(normed_ref[...], weight_halves(place_ref, 0, pieces)).astype(BF16)
    first = low_lanes(tok, size)
    for pair in range(heads // 2):
        lanes = slice(pair * 2 * size, (pair + 1) * 2 * size)
        made = [mm(probs_ref[2 * pair + part], v_ref[:, lanes]) for part in range(2)]
        attended_ref[:, lanes] = jnp.where(first, made[0], made[1]).astype(BF16)
    halves = weight_halves(place_ref, 1, pieces)
    residual = tokens_ref[...].astype(F32) + project(attended_ref[...], halves)
    residual_ref[...] = residual
    factor = lax.rsqrt(jnp.mean(residual * residual, axis=-1, keepdims=True) + EPSILON)
    normed = (residual * factor * gain_ref[...]).astype(BF16)
    normed_two_ref[...] = normed
    probs = router_softmax(normed, router_ref[...], experts)
    lane = lax.broadcasted_iota(jnp.int32, probs.shape, 1)
    gate_ref[...] = jnp.sum(jnp.where(lane == routes_ref[...], probs, 0.0), axis=-1, keepdims=True)


def router_softmax(normed, router, experts):
    logits = mm(normed, router)
    lane = lax.broadcasted_iota(jnp.int32, logits.shape, 1)
    logits = jnp.where(lane < experts, logits, -1e30)
    exponent = jnp.exp(logits - jnp.max(logits, axis=-1, keepdims=True))
    return exponent / jnp.sum(exponent, axis=-1, keepdims=True)


def expert_kernel(
    experts,
    me_ref,
    rows_ref,
    cot_ref,
    router_ref,
    first_ref,
    second_ref,
    back_ref,
    hidden_ref,
    grad_pre_ref,
    produced_ref,
    grad_rows_ref,
    rows_turned_ref,
    cot_turned_ref,
    grad_logits_ref,
    made_ref,
    grad_ref,
    probs_ref,
):
    step, steps = pl.program_id(0), pl.num_programs(0)

    @pl.when(step == 0)
    def _():
        probs_ref[...] = router_softmax(rows_ref[...], router_ref[...], experts)
        rows_turned_ref[...] = rows_ref[...].T

    probs = probs_ref[...]
    chosen = lax.broadcasted_iota(jnp.int32, probs.shape, 1) == me_ref[0]
    gate = jnp.sum(jnp.where(chosen, probs, 0.0), axis=-1, keepdims=True)
    pre_act = mm(rows_ref[...], first_ref[0])
    cdf = 0.5 + 0.5 * lax.erf(pre_act * INV_ROOT_TWO)
    hidden = (pre_act * cdf).astype(BF16)
    slope = cdf + pre_act * jnp.exp(-0.5 * pre_act * pre_act) * INV_ROOT_TWO_PI
    grad_pre = (back_ref[...].astype(F32) * gate * slope).astype(BF16)
    hidden_ref[...] = hidden
    grad_pre_ref[...] = grad_pre
    made = mm(hidden, second_ref[0])
    grad = mm_nt(grad_pre, first_ref[0])

    @pl.when(step == 0)
    def _():
        made_ref[...] = made
        grad_ref[...] = grad

    @pl.when(step > 0)
    def _():
        made_ref[...] += made
        grad_ref[...] += grad

    @pl.when(step == steps - 1)
    def _():
        produced = made_ref[...].astype(BF16)
        produced_ref[...] = produced
        cot = cot_ref[...].astype(F32)
        grad_gate = jnp.sum(cot * produced.astype(F32), axis=-1, keepdims=True)
        grad_logits = (grad_gate * gate * (chosen.astype(F32) - probs)).astype(BF16)
        grad_logits_ref[...] = grad_logits
        grad_rows_ref[...] = (grad_ref[...] + mm_nt(grad_logits, router_ref[...])).astype(BF16)
        cot_turned_ref[...] = (cot * gate).astype(BF16).T


def run_expert(experts, me, rows, cot, router, w_in, w_out, slot_back, part):
    count, width = rows.shape
    inner = w_in.shape[2]
    tile = 512
    lanes = router.shape[1]
    const = lambda shape: pl.BlockSpec(shape, lambda j, s: (0, 0))
    wide = pl.BlockSpec((count, tile), lambda j, s: (0, j))
    return pl.pallas_call(
        functools.partial(expert_kernel, experts),
        out_shape=[
            jax.ShapeDtypeStruct((count, inner), BF16),
            jax.ShapeDtypeStruct((count, inner), BF16),
            jax.ShapeDtypeStruct((count, width), BF16),
            jax.ShapeDtypeStruct((count, width), BF16),
            jax.ShapeDtypeStruct((width, count), BF16),
            jax.ShapeDtypeStruct((width, count), BF16),
            jax.ShapeDtypeStruct((count, lanes), BF16),
        ],
        grid_spec=pltpu.PrefetchScalarGridSpec(
            num_scalar_prefetch=1,
            grid=(inner // tile,),
            in_specs=[
                const((count, width)),
                const((count, width)),
                const((width, lanes)),
                pl.BlockSpec((1, width, tile), lambda j, s: (0, 0, j)),
                pl.BlockSpec((1, tile, width), lambda j, s: (0, j, 0)),
                pl.BlockSpec((count, tile), lambda j, s: (part, j)),
            ],
            out_specs=[wide, wide]
            + [const((count, width))] * 2
            + [const((width, count))] * 2
            + [const((count, lanes))],
            scratch_shapes=[
                pltpu.VMEM((count, width), F32),
                pltpu.VMEM((count, width), F32),
                pltpu.VMEM((count, lanes), F32),
            ],
        ),
        cost_estimate=estimate(9),
        compiler_params=pltpu.CompilerParams(vmem_limit_bytes=VMEM_BYTES),
    )(me, rows, cot, router, w_in, w_out, slot_back)


def outer_kernel(keep, second, place_ref, left_a, left_b, right_a, right_b, *refs):
    total = mm(left_a[...], right_a[...]) + mm(left_b[...], right_b[...])
    if not keep:
        refs[0][0] = total.astype(BF16)
        return
    got, outs = refs[0], refs[1:]
    total = (total + got[0].astype(F32)).astype(BF16)
    step = pl.program_id(0)
    if second:
        half = total.shape[0] // 2
        high = place_ref[0]
        send = jnp.where(high == 0, total[half:], total[:half])
        kept = jnp.where(high == 0, total[:half], total[half:])
        for block in range(len(outs) - 2):

            @pl.when(step == block)
            def _():
                outs[block][0] = send[: half // 2]
                outs[block][1] = kept[: half // 2]

        outs[-2][0] = send[half // 2 :]
        outs[-1][0] = kept[half // 2 :]
        return
    blocks, rows, _ = outs[0].shape
    for part in range(2):

        @pl.when(step == part)
        def _():
            for block in range(blocks):
                at = lax.rem(block - place_ref[2] + blocks, blocks)
                start = 2 * block * rows
                outs[2 * part][at] = total[start : start + rows]
                outs[2 * part + 1][at] = total[start + rows : start + 2 * rows]


def outer_grad(second, place, left, right, blocks, got=None, us=0):
    keep = got is not None
    width, count = left[0].shape
    inner = right[0].shape[1]
    core = lambda s: s[1] if keep else 1 - s[1]
    whole = pl.BlockSpec((width, count), lambda i, s: (0, 0))
    fixed = lambda shape: pl.BlockSpec(shape, lambda i, s: (0,) * len(shape))
    if second:
        steps, columns = blocks, inner // (2 * blocks)
        wide = pl.BlockSpec((count, columns), lambda i, s: (0, 2 * lax.rem(i + s[2], blocks) + core(s)))
        quarter = pl.BlockSpec((1, width // 4, columns), lambda i, s: (i, 0, 0))
        shapes = [(2, width // 4, columns)] * blocks + [(blocks, width // 4, columns)] * 2
        out_specs = [fixed(shapes[0])] * blocks + [quarter] * 2
    else:
        steps, columns = 2, inner // 4
        wide = pl.BlockSpec(
            (count, columns), lambda i, s: (0, 2 * jnp.where(i == 0, 1 - s[0], s[0]) + core(s))
        )
        shapes = [(blocks, width // (2 * blocks), columns)] * 4
        out_specs = [fixed(shapes[0])] * 4
    got_spec = pl.BlockSpec((1, width, columns), lambda i, s: (i, 0, 0))
    if not keep:
        out_specs, shapes = [got_spec], [(steps, width, columns)]
    return pl.pallas_call(
        functools.partial(outer_kernel, keep, second),
        out_shape=[jax.ShapeDtypeStruct(s, BF16) for s in shapes],
        grid_spec=pltpu.PrefetchScalarGridSpec(
            num_scalar_prefetch=1,
            grid=(steps,),
            in_specs=[whole, whole, wide, wide] + ([got_spec] if keep else []),
            out_specs=out_specs,
        ),
        cost_estimate=estimate(us),
        compiler_params=pltpu.CompilerParams(vmem_limit_bytes=VMEM_BYTES),
    )(place, *left, *right, *([got] if keep else []))


def add_kernel(count, *refs):
    ins, outs = refs[: len(refs) - count], refs[len(refs) - count :]
    for index, out in enumerate(outs):
        total = 0.0
        for ref in ins:
            total = total + (ref[index] if count > 1 else ref[...]).astype(F32)
        out[...] = total.astype(BF16)


def add_arrays(arrays, count=1, us=0):
    shape = arrays[0].shape[1:] if count > 1 else arrays[0].shape
    outs = whole_call(functools.partial(add_kernel, count), [(shape, BF16)] * count, [], arrays, us=us)
    return outs if count > 1 else outs[0]


def core_add_kernel(place_ref, keep_ref, got_ref, send_low, send_high, keep_low, keep_high):
    blocks, rows = send_low.shape[1], send_low.shape[2]
    me = place_ref[3]
    for matrix in range(2):
        for block in range(blocks):
            at = lax.rem(block - place_ref[2] + blocks, blocks)
            start = 4 * block * rows
            total = keep_ref[matrix, start : start + 4 * rows].astype(F32)
            total = (total + got_ref[matrix, start : start + 4 * rows].astype(F32)).astype(BF16)
            one, two = total[: 2 * rows], total[2 * rows :]
            mine, other = jnp.where(me == 0, one, two), jnp.where(me == 0, two, one)
            send_low[matrix, at] = other[:rows]
            send_high[matrix, at] = other[rows:]
            keep_low[matrix, at] = mine[:rows]
            keep_high[matrix, at] = mine[rows:]


def pair_add_kernel(place_ref, keep_ref, got_ref, send_ref, mine_ref):
    high = place_ref[0]
    send_ref[...] = (keep_ref[1 - high].astype(F32) + got_ref[1 - high].astype(F32)).astype(BF16)
    mine_ref[...] = (keep_ref[high].astype(F32) + got_ref[high].astype(F32)).astype(BF16)


def lay_rows_kernel(rows, place_ref, own_ref, got_ref, out_ref, *rest):
    blocks = own_ref.shape[0]
    me = place_ref[3]
    for block in range(blocks):
        at = lax.rem(place_ref[2] - block + blocks, blocks)
        own, got = own_ref[at], got_ref[at]
        both = (jnp.where(me == 0, own, got), jnp.where(me == 0, got, own))
        for index in range(2):
            start = (2 * block + index) * rows
            out_ref[start : start + rows, :] = both[index][:rows]
            for ref in rest:
                ref[2 * block + index] = both[index][rows:, : ref.shape[2]]


def attend_back_kernel(
    place_ref,
    mask_ref,
    own_ref,
    got_ref,
    residual_ref,
    cot_ref,
    gain_ref,
    attended_ref,
    *refs,
):
    pieces = refs[:4]
    q_ref, k_ref, v_ref, probs_ref, normed_ref, send_ref, keep_ref, ds_ref, gq_ref, gk_ref, gv_ref = refs[4:15]
    grad_res_ref, gain_grad_ref, ga_ref, gat_ref, qt_ref, kt_ref = refs[15:]
    heads, tok, _ = probs_ref.shape
    size = residual_ref.shape[1] // heads
    low = place_ref[1]

    def store(index, grad):
        grad = grad.astype(BF16)

        @pl.when(low == index % 2)
        def _():
            keep_ref[index // 2] = grad

        @pl.when(low != index % 2)
        def _():
            send_ref[index // 2] = grad

    grad_two = jnp.where(mask_ref[...] > 0, own_ref[...], got_ref[...]).astype(F32)
    residual = residual_ref[...]
    factor = lax.rsqrt(jnp.mean(residual * residual, axis=-1, keepdims=True) + EPSILON)
    scaled = grad_two * gain_ref[...]
    inner = jnp.mean(scaled * residual, axis=-1, keepdims=True)
    grad_res = cot_ref[...].astype(F32) + factor * scaled - residual * (factor * factor * factor) * inner
    grad_res_ref[...] = grad_res
    gain_grad_ref[...] = jnp.sum(grad_two * residual * factor, axis=0, keepdims=True)
    grad_attn = grad_res.astype(BF16)
    store(3, mm(attended_ref[...].T, grad_attn))
    left, right = weight_halves(place_ref, 1, pieces)
    half = left.shape[1]
    ga_ref[...] = (mm_nt(grad_attn[:, :half], left) + mm_nt(grad_attn[:, half:], right)).astype(BF16)
    gat_ref[...] = (mm_nt(left, grad_attn[:, :half]) + mm_nt(right, grad_attn[:, half:])).astype(BF16)
    qt_ref[...] = q_ref[...].T
    kt_ref[...] = k_ref[...].T
    first = low_lanes(tok, size)
    for head in range(heads):
        lanes = slice(head // 2 * 2 * size, (head // 2 + 1) * 2 * size)
        rows = slice(head * size, (head + 1) * size)
        grads = ga_ref[:, lanes]
        picked = jnp.where(first if head % 2 == 0 else ~first, grads, jnp.zeros_like(grads))
        grad_probs = mm_nt(picked, v_ref[:, lanes])
        probs = probs_ref[head]
        wide = probs.astype(F32)
        total = jnp.sum(wide * grad_probs, axis=-1, keepdims=True)
        ds = (wide * (grad_probs - total)).astype(BF16)
        ds_ref[head] = ds
        gq_ref[rows, :] = mm_nt(kt_ref[rows, :], ds).astype(BF16)
        gk_ref[rows, :] = mm(qt_ref[rows, :], ds).astype(BF16)
        gv_ref[rows, :] = mm(gat_ref[rows, :], probs).astype(BF16)
    turned = normed_ref[...].T
    store(0, mm_nt(turned, gq_ref[...]))
    store(1, mm_nt(turned, gk_ref[...]))
    store(2, mm_nt(turned, gv_ref[...]))


def finish_kernel(
    place_ref,
    tokens_ref,
    gain_ref,
    *refs,
):
    qk_pieces, vo_pieces = refs[:4], refs[4:8]
    gq_ref, gk_ref, gv_ref, ds_ref, grad_res_ref, grad_tokens_ref, gain_grad_ref, diag_ref = refs[8:]
    heads, tok, _ = ds_ref.shape
    window = diag_ref.shape[1]
    grad = project_back(gq_ref[...], weight_halves(place_ref, 0, qk_pieces))
    grad = grad + project_back(gk_ref[...], weight_halves(place_ref, 1, qk_pieces))
    grad = grad + project_back(gv_ref[...], weight_halves(place_ref, 0, vo_pieces))
    grad = grad.T
    values = tokens_ref[...].astype(F32)
    factor = lax.rsqrt(jnp.mean(values * values, axis=-1, keepdims=True) + EPSILON)
    scaled = grad * gain_ref[...]
    inner = jnp.mean(scaled * values, axis=-1, keepdims=True)
    grad_tokens_ref[...] = grad_res_ref[...] + factor * scaled - values * (factor * factor * factor) * inner
    gain_grad_ref[...] = jnp.sum(grad * values * factor, axis=0, keepdims=True)
    row = lax.broadcasted_iota(jnp.int32, (tok, tok), 0)
    column = lax.broadcasted_iota(jnp.int32, (tok, tok), 1)
    turned = (row + column == tok - 1).astype(BF16)
    for head in range(heads):
        flipped = mm(turned, ds_ref[head])
        wide = jnp.concatenate([flipped, jnp.zeros((tok, window - tok), F32)], axis=1)
        rolled = pltpu.roll(wide, window - tok + 1, 1, stride=1, stride_axis=0)
        diag_ref[head : head + 1, :] = jnp.sum(rolled, axis=0, keepdims=True)


def second_shared_kernel(place_ref, *refs):
    pieces, out = refs[:4], refs[4]
    rows, columns = pieces[0].shape
    for target in range(4):
        x, core = target // 2, target % 2
        out[0, core * rows : (core + 1) * rows, x * columns : (x + 1) * columns] = choose(place_ref, target, pieces).astype(F32)


def first_shared_kernel(place_ref, *refs):
    pieces, out = refs[:4], refs[4]
    columns = pieces[0].shape[1]
    for target in range(4):
        out[0, :, target * columns : (target + 1) * columns] = choose(place_ref, target, pieces).astype(F32)


def attention_shared_kernel(place_ref, *refs):
    for target in range(4):
        refs[4 + target][...] = choose(place_ref, target, refs[:4]).astype(F32)


def spread(values, *others):
    far = rep_swap(values, 2)
    if others:
        far = after(far, *others)
    return [values, rep_swap(values, 1), far, rep_swap(far, 1)]


def after(values, *others):
    return lax.optimization_barrier((values,) + others)[0]


def local(
    tokens,
    doc_ids,
    routes,
    cotangent,
    attn_gain,
    w_query,
    w_key,
    w_value,
    w_output,
    rel_table,
    ffn_gain,
    w_router,
    w_in,
    w_out,
):
    tok_rows, width = tokens.shape
    head_count = rel_table.shape[1]
    experts = w_router.shape[1]
    dp_count = lax.axis_size("dp")
    expert_axis = lax.axis_size("expert")
    capacity = 2 * tok_rows // expert_axis
    inner = w_in.shape[2]
    rep = lax.axis_index("rep")
    high, low = rep // 2, rep % 2
    me = lax.axis_index("expert")
    dp = lax.axis_index("dp")
    place = jnp.stack([high, low, dp, me]).astype(jnp.int32)
    shard_rows = w_query.shape[0]
    lanes = 128
    slots = experts * capacity

    onehot = bucket_onehot(tok_rows, rel_table.shape[0])
    diag_values = jnp.dot(onehot, rel_table, precision=lax.Precision.HIGHEST).T
    square = (head_count, tok_rows, tok_rows)
    (bias,) = whole_call(
        bias_kernel, [(square, F32)], [], [diag_values, doc_ids[None, :], doc_ids[:, None]], us=2
    )

    half = width // 2
    small = jnp.concatenate([attn_gain[None], ffn_gain[None], w_router.T], axis=0)
    small_rows = -(-(2 + experts) // 16) * 16
    small = jnp.pad(small, ((0, small_rows - 2 - experts), (0, half - shard_rows)))

    def quarter(one, two):
        return lax.dynamic_slice_in_dim(jnp.where(high == 0, one, two), low * half, half, 1)

    qk_quarter = jnp.concatenate([quarter(w_query, w_key), small], axis=0)
    vo_quarter = quarter(w_value, w_output)
    if expert_axis == 2:

        def along_dp(values):
            return jnp.stack([values] + [shift(values, "dp", step) for step in range(1, dp_count)])

        qk_own, vo_own = along_dp(qk_quarter), along_dp(vo_quarter)
        qk_own = after(qk_own, bias)
        qk_got = shift(qk_own, "expert", 1)
        vo_got = shift(vo_own, "expert", 1)
        rest_shape = (dp_count * expert_axis, small_rows, lanes)
        qk_mine, rest = whole_call(
            functools.partial(lay_rows_kernel, shard_rows),
            [((width, half), BF16), (rest_shape, BF16)],
            [place],
            [qk_own, qk_got],
            us=1,
        )
        (vo_mine,) = whole_call(
            functools.partial(lay_rows_kernel, shard_rows), [((width, half), BF16)], [place], [vo_own, vo_got], us=1
        )
    else:
        rows_all = lax.all_gather(qk_quarter, ("dp", "expert"), axis=0)
        qk_mine, rest = rows_all[:, :shard_rows].reshape(width, half), rows_all[:, shard_rows:]
        vo_mine = lax.all_gather(vo_quarter, ("dp", "expert"), axis=0, tiled=True)
    rest = jnp.moveaxis(rest[:, : 2 + experts, :shard_rows], 1, 0).reshape(2 + experts, width)
    gain_one = rest[0:1].astype(F32)
    gain_two = rest[1:2].astype(F32)
    router = jnp.pad(rest[2:].T, ((0, 0), (0, lanes - experts)))
    qk_pieces = spread(qk_mine)

    route_ids = routes[:, 0]
    direct = expert_axis == 2 and capacity == tok_rows
    if direct:
        own_mask = (routes == me).astype(F32)

        def send(values):
            return values, shift(values, "expert", 1)

        def back(one, two):
            return one, shift(two, "expert", 1)

        zero = jnp.zeros_like(cotangent)
        cot_a = jnp.where(routes == me, cotangent, zero)
        cot_b = shift(after(jnp.where(routes == me, zero, cotangent), vo_got), "expert", 1)
    else:
        own_mask = jnp.ones((tok_rows, 1), F32)
        chosen = (route_ids[:, None] == jnp.arange(experts, dtype=jnp.int32)[None, :]).astype(jnp.int32)
        slot_rank = jnp.sum(jnp.cumsum(chosen, axis=0) * chosen, axis=-1) - 1
        slot_index = route_ids * capacity + slot_rank
        place_of = (jnp.arange(slots, dtype=jnp.int32)[:, None] == slot_index[None, :]).astype(BF16)

        def send(values):
            filled = mm(place_of, values).astype(BF16)
            filled = lax.all_to_all(filled, "expert", split_axis=0, concat_axis=0, tiled=True)
            return filled[: slots // 2], filled[slots // 2 :]

        def back(one, two):
            rows = jnp.concatenate([one, two], axis=0)
            rows = lax.all_to_all(rows, "expert", split_axis=0, concat_axis=0, tiled=True)
            rows = mm_tn(place_of, rows).astype(BF16)
            return rows, rows

        cot_a, cot_b = send(cotangent)

    slot_back = mm_nt(jnp.concatenate([cot_a, cot_b], axis=0), w_out[0]).astype(BF16)

    flat = (tok_rows, width)
    normed_one, queries, keys, probs = whole_call(
        scores_kernel,
        [(flat, BF16)] * 3 + [(square, BF16)],
        [place],
        [tokens, gain_one, *qk_pieces, bias],
        us=4,
    )
    vo_pieces = spread(vo_mine, slot_back, normed_one)
    values, attended, residual, normed_two, gate = whole_call(
        functools.partial(attend_kernel, experts),
        [(flat, BF16), (flat, BF16), (flat, F32), (flat, BF16), ((tok_rows, 1), F32)],
        [place],
        [tokens, normed_one, gain_two, router, routes, *vo_pieces, probs],
        us=4,
    )

    rows_a, rows_b = send(normed_two)
    where_me = me[None].astype(jnp.int32)
    run = functools.partial(run_expert, experts, where_me)
    hid_a, pre_a, made_a, grad_a, turn_a, cot_turn_a, logits_a = run(
        rows_a, cot_a, router, w_in, w_out, slot_back, 0
    )
    hid_b, pre_b, made_b, grad_b, turn_b, cot_turn_b, logits_b = run(
        rows_b, cot_b, router, w_in, w_out, slot_back, 1
    )
    grad_own, grad_got = back(grad_a, grad_b)

    hid, pre, rows, cots = (hid_a, hid_b), (pre_a, pre_b), (turn_a, turn_b), (cot_turn_a, cot_turn_b)
    (second_out,) = outer_grad(True, place, cots, hid, dp_count, us=BIG)
    second_in = rep_swap(second_out, 1)
    (first_out,) = outer_grad(False, place, rows, pre, dp_count)
    first_in = rep_swap(first_out, 1)
    *early, second_send, second_keep = outer_grad(True, place, cots, hid, dp_count, second_in)
    first_in = after(first_in, grad_got, second_send)
    first_send, first_late, first_keep, first_last = outer_grad(False, place, rows, pre, dp_count, first_in, us=BIG)
    grad_got = after(grad_got, second_send, first_send)

    def z_sent(blocks):
        return [blocks[0]] + [shift(blocks[step], "dp", step) for step in range(1, dp_count)]

    early = z_sent(early)
    second_got = rep_swap(second_send, 2)

    square_weight = (2, width, width)
    send_part, keep_part, grad_scores, grad_q, grad_k, grad_v, grad_res, grad_gain_two = whole_call(
        attend_back_kernel,
        [(square_weight, BF16)] * 2
        + [(square, BF16)]
        + [((width, tok_rows), BF16)] * 3
        + [(flat, F32), ((1, width), F32)],
        [place],
        [own_mask, grad_own, grad_got, residual, cotangent, gain_two, attended]
        + [*vo_pieces, queries, keys, values, probs, normed_one],
        scratch=[pltpu.VMEM(flat, BF16)] + [pltpu.VMEM((width, tok_rows), BF16)] * 3,
        us=0,
    )
    core_got = rep_swap(send_part, 1)

    second_blocks = list(add_arrays([after(second_keep, grad_res), second_got], dp_count))
    first_got = rep_swap(after(first_send, second_got), 2)

    grad_tokens, grad_gain_one, diag_grads = whole_call(
        finish_kernel,
        [(flat, F32), ((1, width), F32), ((head_count, 2 * tok_rows), F32)],
        [place],
        [tokens, gain_one, *qk_pieces, *vo_pieces, grad_q, grad_k, grad_v, grad_scores]
        + [after(grad_res, second_blocks[0])],
        us=0,
    )

    early_sum = add_arrays([after(early[0], grad_tokens)] + early[1:], us=BIG)
    early_got = rep_swap(early_sum[0], 2)
    second_blocks[0] = after(second_blocks[0], early_sum)
    second_z = z_sent([second_blocks[0]] + [after(block, early_sum) for block in second_blocks[1:]])

    keep_part = after(keep_part, early_sum)
    if expert_axis == 2:
        rows_half = shard_rows // 2
        chunk_shape = (2, dp_count, rows_half, width)
        send_low, send_high, keep_low, keep_high = whole_call(
            core_add_kernel, [(chunk_shape, BF16)] * 4, [place], [keep_part, core_got], us=2
        )
        low_got = shift(send_low, "expert", 1)
        token = send_low
    else:
        part = add_pair(keep_part, core_got).reshape(2, dp_count, expert_axis, shard_rows, width)
        part = sum_over(part, "expert", 2)
        token = part

    first_blocks = add_arrays([after(first_keep, token), first_got], dp_count)
    first_z = z_sent(first_blocks)
    late_got = rep_swap(after(first_late, first_got), 2)

    if expert_axis == 2:
        pair_shape = [(chunk_shape[1:], BF16)] * 2
        x_send, x_low = whole_call(
            pair_add_kernel, pair_shape, [place], [after(keep_low, first_blocks[0]), low_got], us=1
        )
        high_got = shift(after(send_high, low_got), "expert", 1)
        x_low_got = rep_swap(x_send, 2)
        token = x_low

    late_blocks = add_arrays([after(first_last, token), late_got], dp_count)
    late_z = z_sent(late_blocks)

    second_low = add_arrays([after(second_z[0], late_blocks[0])] + second_z[1:])
    second_high = add_arrays([after(early_sum[1], second_low), early_got])
    second_pieces = spread(jnp.concatenate([second_high, second_low], axis=0).T)

    if expert_axis == 2:
        low_blocks = add_arrays([after(x_low, second_pieces[0]), x_low_got], dp_count)
        low_z = z_sent(low_blocks)
        x_send, x_high = whole_call(
            pair_add_kernel, pair_shape, [place], [after(keep_high, low_blocks[0]), high_got], us=1
        )
        x_high_got = rep_swap(x_send, 2)
        first_low = add_arrays([after(first_z[0], x_high)] + first_z[1:])
        high_blocks = add_arrays([after(x_high, first_low), x_high_got], dp_count)
        high_z = z_sent(high_blocks)
        token = x_high
        first_high = add_arrays([after(late_z[0], high_blocks[0])] + late_z[1:])
        first_pieces = spread(jnp.concatenate([first_low, first_high], axis=0))
        attn_low = add_arrays([after(low_z[0], first_pieces[0])] + low_z[1:])
        attn_high = add_arrays([after(high_z[0], attn_low)] + high_z[1:])
        attn_pieces = spread(jnp.concatenate([attn_low, attn_high], axis=0))
    else:
        first_low = add_arrays([first_z[0]] + first_z[1:])
        first_high = add_arrays([late_z[0]] + late_z[1:])
        first_pieces = spread(jnp.concatenate([first_low, first_high], axis=0))
        x_part = add_pair(pick(part, high, 0), rep_swap(pick(part, 1 - high, 0), 2))
        attn_pieces = spread(sum_over(x_part, "dp", 0))
        token = x_part
    (grad_w_out,) = whole_call(
        second_shared_kernel, [((1, inner // dp_count, width), F32)], [place], second_pieces
    )
    (grad_w_in,) = whole_call(first_shared_kernel, [((1, width // dp_count, inner), F32)], [place], first_pieces)
    owned = whole_call(attention_shared_kernel, [((shard_rows, width), F32)] * 4, [place], attn_pieces)

    made_own, made_got = back(made_a, after(made_b, token))
    expert_rows = jnp.where(own_mask > 0, made_own, made_got).astype(F32)
    mixed = (residual + gate * expert_rows).astype(BF16)
    grad_router = mm(turn_a, logits_a) + mm(turn_b, logits_b)
    grad_router = grad_router[:, :experts]
    grad_table = jnp.dot(onehot.T, diag_grads.T, precision=lax.Precision.HIGHEST)
    small = jnp.concatenate([grad_gain_one, grad_gain_two, grad_router.T], axis=0)
    packed = jnp.concatenate([small.reshape(-1), grad_table.reshape(-1)])
    packed = all_sum(packed, (early_sum, first_blocks[0], late_blocks[0]))
    row_start = (dp * expert_axis + me) * shard_rows
    small = packed[: (2 + experts) * width].reshape(2 + experts, width)
    small = lax.dynamic_slice_in_dim(small, row_start, shard_rows, 1)
    table_total = packed[(2 + experts) * width :].reshape(rel_table.shape)
    return (
        mixed,
        grad_tokens,
        small[0],
        owned[0],
        owned[1],
        owned[2],
        owned[3],
        table_total,
        small[1],
        small[2:].T,
        grad_w_in,
        grad_w_out,
    )


def all_sum(values, tokens):
    for axis, token in zip(("rep", "expert", "dp"), tokens, strict=True):
        count = lax.axis_size(axis)
        if count > 4:
            values = lax.psum(values, axis)
            continue
        total = values = after(values, token)
        for step in range(1, count):
            total = total + shift(values, axis, step)
        values = total
    return values


def solution(mesh):
    rows = P(("rep", "dp", "expert"), None)
    split = P(("dp", "expert"), None)
    vector = P(("dp", "expert"))
    return jax.shard_map(
        local,
        mesh=mesh,
        in_specs=(
            rows,
            P(("rep", "dp", "expert")),
            rows,
            rows,
            vector,
            split,
            split,
            split,
            split,
            P(),
            vector,
            split,
            P("expert", None, None),
            P("expert", None, None),
        ),
        out_specs=(
            rows,
            rows,
            vector,
            split,
            split,
            split,
            split,
            P(),
            vector,
            split,
            P("expert", "dp", None),
            P("expert", "dp", None),
        ),
        check_vma=False,
    )
```

```python
import functools

import jax
import jax.numpy as jnp
from jax import lax
from jax.experimental import pallas as pl
from jax.experimental.pallas import tpu as pltpu
from jax.sharding import PartitionSpec as P

EPSILON = 1e-06
BUCKET_BOUNDS = (12, 16, 23, 32, 46, 64, 91)
INV_ROOT_TWO = 0.7071067811865476
INV_ROOT_TWO_PI = 0.3989422804014327
BF16 = jnp.bfloat16
F32 = jnp.float32


def bucket_of(offsets):
    distance = jnp.abs(offsets)
    levels = jnp.minimum(distance, 8)
    for threshold in BUCKET_BOUNDS:
        levels = levels + (distance >= threshold).astype(jnp.int32)
    return levels + 16 * (offsets > 0).astype(jnp.int32)


def bucket_onehot(tok_rows, bucket_count):
    window = 2 * tok_rows
    places = jnp.arange(window, dtype=jnp.int32)
    offsets = jnp.where(places < tok_rows, places, places - window)
    return (
        bucket_of(offsets)[:, None] == jnp.arange(bucket_count, dtype=jnp.int32)[None, :]
    ).astype(F32)


def rep_swap(values, bit):
    count = lax.axis_size("rep")
    return lax.ppermute(values, "rep", [(i, i ^ bit) for i in range(count)])


def shift(values, axis, step):
    count = lax.axis_size(axis)
    return lax.ppermute(values, axis, [(i, (i + step) % count) for i in range(count)])


def pick(values, index, axis):
    return lax.dynamic_index_in_dim(values, index, axis, keepdims=False)


def add_pair(one, two):
    return (one.astype(F32) + two.astype(F32)).astype(BF16)


def sum_over(values, axis, dimension):
    total = lax.psum_scatter(values.astype(F32), axis, scatter_dimension=dimension, tiled=False)
    return total.astype(BF16)


VMEM_BYTES = 26 * 1024 * 1024
EXPERT_VMEM = 18 * 1024 * 1024
BIG = 30
NT = (((1,), (1,)), ((), ()))
TN = (((0,), (0,)), ((), ()))


def mm(one, two):
    return jnp.dot(one, two, preferred_element_type=F32)


def mm_nt(one, two):
    return lax.dot_general(one, two, NT, preferred_element_type=F32)


def mm_tn(one, two):
    return lax.dot_general(one, two, TN, preferred_element_type=F32)


def estimate(us):
    return pl.CostEstimate(flops=us * 10**9 + 1, bytes_accessed=us * 10**6 + 1, transcendentals=0)


def whole_call(kernel, outs, scalars, arrays, scratch=(), us=2, vmem_bytes=VMEM_BYTES):
    vmem = pl.BlockSpec(memory_space=pltpu.VMEM)
    return pl.pallas_call(
        kernel,
        out_shape=[jax.ShapeDtypeStruct(s, d) for s, d in outs],
        in_specs=[pl.BlockSpec(memory_space=pltpu.SMEM)] * len(scalars) + [vmem] * len(arrays),
        out_specs=[vmem] * len(outs),
        scratch_shapes=list(scratch),
        cost_estimate=estimate(us),
        compiler_params=pltpu.CompilerParams(vmem_limit_bytes=vmem_bytes),
    )(*scalars, *arrays)


def bias_kernel(diag_ref, row_ref, col_ref, bias_ref):
    heads, tok, _ = bias_ref.shape
    window = diag_ref.shape[1]
    same = row_ref[...] == col_ref[...]
    for head in range(heads):
        wide = jnp.broadcast_to(diag_ref[head : head + 1, :], (tok, window))
        rolled = pltpu.roll(wide, 0, 1, stride=1, stride_axis=0)
        bias_ref[head] = jnp.where(same, rolled[:, :tok], -1e30)


def choose(place_ref, target, pieces):
    at = jnp.bitwise_xor(2 * place_ref[0] + place_ref[1], target)
    near = jnp.where(at % 2 == 0, pieces[0][...], pieces[1][...])
    far = jnp.where(at % 2 == 0, pieces[2][...], pieces[3][...])
    return jnp.where(at < 2, near, far)


def weight_halves(place_ref, index, pieces):
    return choose(place_ref, 2 * index, pieces), choose(place_ref, 2 * index + 1, pieces)


def project(values, halves):
    return jnp.concatenate([mm(values, halves[0]), mm(values, halves[1])], axis=1)


def project_back(turned, halves):
    half = turned.shape[0] // 2
    return mm(halves[0], turned[:half]) + mm(halves[1], turned[half:])


def low_lanes(tok, head_size):
    return lax.broadcasted_iota(jnp.int32, (tok, 2 * head_size), 1) < head_size


def scores_kernel(place_ref, tokens_ref, gain_ref, *refs):
    pieces = refs[:4]
    bias_ref, normed_ref, q_ref, k_ref, probs_ref = refs[4:]
    heads, tok, _ = bias_ref.shape
    size = tokens_ref.shape[1] // heads
    values = tokens_ref[...].astype(F32)
    factor = lax.rsqrt(jnp.mean(values * values, axis=-1, keepdims=True) + EPSILON)
    normed = (values * factor * gain_ref[...]).astype(BF16)
    normed_ref[...] = normed
    q_ref[...] = project(normed, weight_halves(place_ref, 0, pieces)).astype(BF16)
    k_ref[...] = project(normed, weight_halves(place_ref, 1, pieces)).astype(BF16)
    first = low_lanes(tok, size)
    for pair in range(heads // 2):
        lanes = slice(pair * 2 * size, (pair + 1) * 2 * size)
        queries, keys = q_ref[:, lanes], k_ref[:, lanes]
        for part in range(2):
            head = 2 * pair + part
            picked = jnp.where(first if part == 0 else ~first, queries, jnp.zeros_like(queries))
            scores = mm_nt(picked, keys) + bias_ref[head]
            exponent = jnp.exp(scores - jnp.max(scores, axis=-1, keepdims=True))
            probs = exponent / jnp.sum(exponent, axis=-1, keepdims=True)
            probs_ref[head] = probs.astype(BF16)


def attend_kernel(
    experts,
    place_ref,
    tokens_ref,
    normed_ref,
    gain_ref,
    router_ref,
    routes_ref,
    *refs,
):
    pieces = refs[:4]
    probs_ref, v_ref, attended_ref, residual_ref, normed_two_ref, gate_ref = refs[4:]
    heads, tok, _ = probs_ref.shape
    size = tokens_ref.shape[1] // heads
    v_ref[...] = project(normed_ref[...], weight_halves(place_ref, 0, pieces)).astype(BF16)
    first = low_lanes(tok, size)
    for pair in range(heads // 2):
        lanes = slice(pair * 2 * size, (pair + 1) * 2 * size)
        made = [mm(probs_ref[2 * pair + part], v_ref[:, lanes]) for part in range(2)]
        attended_ref[:, lanes] = jnp.where(first, made[0], made[1]).astype(BF16)
    halves = weight_halves(place_ref, 1, pieces)
    residual = tokens_ref[...].astype(F32) + project(attended_ref[...], halves)
    residual_ref[...] = residual
    factor = lax.rsqrt(jnp.mean(residual * residual, axis=-1, keepdims=True) + EPSILON)
    normed = (residual * factor * gain_ref[...]).astype(BF16)
    normed_two_ref[...] = normed
    probs = router_softmax(normed, router_ref[...], experts)
    lane = lax.broadcasted_iota(jnp.int32, probs.shape, 1)
    gate_ref[...] = jnp.sum(jnp.where(lane == routes_ref[...], probs, 0.0), axis=-1, keepdims=True)


def router_softmax(normed, router, experts):
    logits = mm(normed, router)
    lane = lax.broadcasted_iota(jnp.int32, logits.shape, 1)
    logits = jnp.where(lane < experts, logits, -1e30)
    exponent = jnp.exp(logits - jnp.max(logits, axis=-1, keepdims=True))
    return exponent / jnp.sum(exponent, axis=-1, keepdims=True)


def expert_kernel(
    experts,
    me_ref,
    rows_ref,
    cot_ref,
    router_ref,
    first_ref,
    second_ref,
    back_ref,
    hidden_ref,
    grad_pre_ref,
    produced_ref,
    grad_rows_ref,
    rows_turned_ref,
    cot_turned_ref,
    grad_logits_ref,
    made_ref,
    grad_ref,
    probs_ref,
):
    step, steps = pl.program_id(0), pl.num_programs(0)

    @pl.when(step == 0)
    def _():
        probs_ref[...] = router_softmax(rows_ref[...], router_ref[...], experts)
        rows_turned_ref[...] = rows_ref[...].T

    probs = probs_ref[...]
    chosen = lax.broadcasted_iota(jnp.int32, probs.shape, 1) == me_ref[0]
    gate = jnp.sum(jnp.where(chosen, probs, 0.0), axis=-1, keepdims=True)
    pre_act = mm(rows_ref[...], first_ref[0])
    cdf = 0.5 + 0.5 * lax.erf(pre_act * INV_ROOT_TWO)
    hidden = (pre_act * cdf).astype(BF16)
    slope = cdf + pre_act * jnp.exp(-0.5 * pre_act * pre_act) * INV_ROOT_TWO_PI
    grad_pre = (back_ref[...].astype(F32) * gate * slope).astype(BF16)
    hidden_ref[...] = hidden
    grad_pre_ref[...] = grad_pre
    made = mm(hidden, second_ref[0])
    grad = mm_nt(grad_pre, first_ref[0])

    @pl.when(step == 0)
    def _():
        made_ref[...] = made
        grad_ref[...] = grad

    @pl.when(step > 0)
    def _():
        made_ref[...] += made
        grad_ref[...] += grad

    @pl.when(step == steps - 1)
    def _():
        produced = made_ref[...].astype(BF16)
        produced_ref[...] = produced
        cot = cot_ref[...].astype(F32)
        grad_gate = jnp.sum(cot * produced.astype(F32), axis=-1, keepdims=True)
        grad_logits = (grad_gate * gate * (chosen.astype(F32) - probs)).astype(BF16)
        grad_logits_ref[...] = grad_logits
        grad_rows_ref[...] = (grad_ref[...] + mm_nt(grad_logits, router_ref[...])).astype(BF16)
        cot_turned_ref[...] = (cot * gate).astype(BF16).T


def run_expert(experts, me, rows, cot, router, w_in, w_out, slot_back, part):
    count, width = rows.shape
    inner = w_in.shape[2]
    tile = 1024
    lanes = router.shape[1]
    const = lambda shape: pl.BlockSpec(shape, lambda j, s: (0, 0))
    wide = pl.BlockSpec((count, tile), lambda j, s: (0, j))
    return pl.pallas_call(
        functools.partial(expert_kernel, experts),
        out_shape=[
            jax.ShapeDtypeStruct((count, inner), BF16),
            jax.ShapeDtypeStruct((count, inner), BF16),
            jax.ShapeDtypeStruct((count, width), BF16),
            jax.ShapeDtypeStruct((count, width), BF16),
            jax.ShapeDtypeStruct((width, count), BF16),
            jax.ShapeDtypeStruct((width, count), BF16),
            jax.ShapeDtypeStruct((count, lanes), BF16),
        ],
        grid_spec=pltpu.PrefetchScalarGridSpec(
            num_scalar_prefetch=1,
            grid=(inner // tile,),
            in_specs=[
                const((count, width)),
                const((count, width)),
                const((width, lanes)),
                pl.BlockSpec((1, width, tile), lambda j, s: (0, 0, j)),
                pl.BlockSpec((1, tile, width), lambda j, s: (0, j, 0)),
                pl.BlockSpec((count, tile), lambda j, s: (part, j)),
            ],
            out_specs=[wide, wide]
            + [const((count, width))] * 2
            + [const((width, count))] * 2
            + [const((count, lanes))],
            scratch_shapes=[
                pltpu.VMEM((count, width), F32),
                pltpu.VMEM((count, width), F32),
                pltpu.VMEM((count, lanes), F32),
            ],
        ),
        cost_estimate=estimate(9),
        compiler_params=pltpu.CompilerParams(vmem_limit_bytes=EXPERT_VMEM),
    )(me, rows, cot, router, w_in, w_out, slot_back)


def outer_kernel(place_ref, *refs):
    cots, hidden, rows, grad_pre = refs[0:2], refs[2:4], refs[4:6], refs[6:8]
    second_send, second_own, first_send, first_own = refs[8:]
    high, low, dp = place_ref[0], place_ref[1], place_ref[2]
    blocks, _, columns = second_send.shape
    for block in range(blocks):
        for core, out in ((1 - low, second_send), (low, second_own)):
            start = (2 * lax.rem(block + dp, blocks) + core) * columns
            lanes = pl.ds(pl.multiple_of(start, 128), columns)
            out[block] = (mm(cots[0][...], hidden[0][:, lanes]) + mm(cots[1][...], hidden[1][:, lanes])).astype(BF16)
    columns = first_send.shape[2]
    for index, x in enumerate((1 - high, high)):
        for core, out in ((1 - low, first_send), (low, first_own)):
            lanes = pl.ds(pl.multiple_of((2 * x + core) * columns, 128), columns)
            out[index] = (mm(rows[0][...], grad_pre[0][:, lanes]) + mm(rows[1][...], grad_pre[1][:, lanes])).astype(BF16)


def core_sum_kernel(place_ref, second_own, second_got, first_own, first_got, *outs):
    high, dp = place_ref[0], place_ref[2]
    blocks, width, _ = second_own.shape
    half, rows = width // 2, width // 4
    for block in range(blocks):
        total = (second_own[block].astype(F32) + second_got[block].astype(F32)).astype(BF16)
        send = jnp.where(high == 0, total[half:], total[:half])
        kept = jnp.where(high == 0, total[:half], total[half:])
        outs[block][0] = send[:rows]
        outs[block][1] = kept[:rows]
        at = lax.rem(block + dp, blocks)
        outs[blocks][at] = send[rows:]
        outs[blocks + 1][at] = kept[rows:]
    rows = width // blocks
    for index in range(2):
        for block in range(blocks):
            lines = slice(block * rows, (block + 1) * rows)
            total = first_own[index, lines].astype(F32) + first_got[index, lines].astype(F32)
            outs[blocks + 2 + index][lax.rem(block - dp + blocks, blocks)] = total.astype(BF16)


def add_kernel(count, *refs):
    ins, outs = refs[: len(refs) - count], refs[len(refs) - count :]
    for index, out in enumerate(outs):
        total = 0.0
        for ref in ins:
            total = total + (ref[index] if count > 1 else ref[...]).astype(F32)
        out[...] = total.astype(BF16)


def add_arrays(arrays, count=1, us=BIG):
    shape = arrays[0].shape[1:] if count > 1 else arrays[0].shape
    outs = whole_call(functools.partial(add_kernel, count), [(shape, BF16)] * count, [], arrays, us=us)
    return outs if count > 1 else outs[0]


def core_add_kernel(place_ref, keep_ref, got_ref, small_ref, small_got_ref, send_ref, mine_ref):
    blocks = send_ref.shape[1]
    rows = keep_ref.shape[1] // (2 * blocks)
    me = place_ref[3]
    for block in range(blocks):
        small = [
            (small_ref[2 * block + at].astype(F32) + small_got_ref[2 * block + at].astype(F32)).astype(BF16)
            for at in range(2)
        ]
        for matrix in range(2):
            start = 2 * block * rows
            total = keep_ref[matrix, start : start + 2 * rows].astype(F32)
            total = (total + got_ref[matrix, start : start + 2 * rows].astype(F32)).astype(BF16)
            one, two = total[:rows], total[rows:]
            mine_ref[matrix, block, :rows] = jnp.where(me == 0, one, two)
            send_ref[matrix, block, :rows] = jnp.where(me == 0, two, one)
            mine_ref[matrix, block, rows:] = jnp.where(me == 0, small[0], small[1])
            send_ref[matrix, block, rows:] = jnp.where(me == 0, small[1], small[0])


def pair_add_kernel(place_ref, keep_ref, got_ref, send_ref, mine_ref):
    high = place_ref[0]
    send_ref[...] = (keep_ref[1 - high].astype(F32) + got_ref[1 - high].astype(F32)).astype(BF16)
    mine_ref[...] = (keep_ref[high].astype(F32) + got_ref[high].astype(F32)).astype(BF16)


def plain_add_kernel(one, two, out):
    out[...] = (one[...].astype(F32) + two[...].astype(F32)).astype(BF16)


def sum_kernel(blocks, out):
    total = blocks[0].astype(F32)
    for block in range(1, blocks.shape[0]):
        total = total + blocks[block].astype(F32)
    out[...] = total.astype(BF16)


def second_sum_kernel(early_keep, early_got, blocks, out):
    low = blocks[0].astype(F32)
    for block in range(1, blocks.shape[0]):
        low = low + blocks[block].astype(F32)
    high = early_keep[1].astype(F32) + early_got[...].astype(F32)
    out[...] = jnp.concatenate([high, low], axis=0).T.astype(BF16)


def lay_rows_kernel(rows, place_ref, own_ref, got_ref, out_ref, *rest):
    blocks = own_ref.shape[0]
    me = place_ref[3]
    for block in range(blocks):
        at = lax.rem(place_ref[2] - block + blocks, blocks)
        own, got = own_ref[at], got_ref[at]
        both = (jnp.where(me == 0, own, got), jnp.where(me == 0, got, own))
        for index in range(2):
            start = (2 * block + index) * rows
            out_ref[start : start + rows, :] = both[index][:rows]
            for ref in rest:
                ref[2 * block + index] = both[index][rows:, : ref.shape[2]]


def attend_back_kernel(
    place_ref,
    mask_ref,
    own_ref,
    got_ref,
    residual_ref,
    cot_ref,
    gain_ref,
    attended_ref,
    *refs,
):
    pieces = refs[:4]
    q_ref, k_ref, v_ref, probs_ref, normed_ref, keep_ref, ds_ref, gq_ref, gk_ref, gv_ref = refs[4:14]
    grad_res_ref, gain_grad_ref, send_ref, ga_ref, gat_ref, qt_ref, kt_ref = refs[14:]
    heads, tok, _ = probs_ref.shape
    size = residual_ref.shape[1] // heads
    low = place_ref[1]

    def store(index, grad):
        grad = grad.astype(BF16)

        @pl.when(low == index % 2)
        def _():
            keep_ref[index // 2] = grad

        @pl.when(low != index % 2)
        def _():
            send_ref[index // 2] = grad

    grad_two = jnp.where(mask_ref[...] > 0, own_ref[...], got_ref[...]).astype(F32)
    residual = residual_ref[...]
    factor = lax.rsqrt(jnp.mean(residual * residual, axis=-1, keepdims=True) + EPSILON)
    scaled = grad_two * gain_ref[...]
    inner = jnp.mean(scaled * residual, axis=-1, keepdims=True)
    grad_res = cot_ref[...].astype(F32) + factor * scaled - residual * (factor * factor * factor) * inner
    grad_res_ref[...] = grad_res
    gain_grad_ref[...] = jnp.sum(grad_two * residual * factor, axis=0, keepdims=True)
    grad_attn = grad_res.astype(BF16)
    store(3, mm(attended_ref[...].T, grad_attn))
    left, right = weight_halves(place_ref, 1, pieces)
    half = left.shape[1]
    ga_ref[...] = (mm_nt(grad_attn[:, :half], left) + mm_nt(grad_attn[:, half:], right)).astype(BF16)
    gat_ref[...] = (mm_nt(left, grad_attn[:, :half]) + mm_nt(right, grad_attn[:, half:])).astype(BF16)
    qt_ref[...] = q_ref[...].T
    kt_ref[...] = k_ref[...].T
    first = low_lanes(tok, size)
    for head in range(heads):
        lanes = slice(head // 2 * 2 * size, (head // 2 + 1) * 2 * size)
        rows = slice(head * size, (head + 1) * size)
        grads = ga_ref[:, lanes]
        picked = jnp.where(first if head % 2 == 0 else ~first, grads, jnp.zeros_like(grads))
        grad_probs = mm_nt(picked, v_ref[:, lanes])
        probs = probs_ref[head]
        wide = probs.astype(F32)
        total = jnp.sum(wide * grad_probs, axis=-1, keepdims=True)
        ds = (wide * (grad_probs - total)).astype(BF16)
        ds_ref[head] = ds
        gq_ref[rows, :] = mm_nt(kt_ref[rows, :], ds).astype(BF16)
        gk_ref[rows, :] = mm(qt_ref[rows, :], ds).astype(BF16)
        gv_ref[rows, :] = mm(gat_ref[rows, :], probs).astype(BF16)
    turned = normed_ref[...].T
    store(0, mm_nt(turned, gq_ref[...]))
    store(1, mm_nt(turned, gk_ref[...]))
    store(2, mm_nt(turned, gv_ref[...]))


def finish_kernel(
    place_ref,
    tokens_ref,
    gain_ref,
    *refs,
):
    qk_pieces, vo_pieces = refs[:4], refs[4:8]
    gq_ref, gk_ref, gv_ref, ds_ref, grad_res_ref, gain_two_ref, onehot_ref = refs[8:15]
    turn_a_ref, turn_b_ref, logits_a_ref, logits_b_ref, grad_tokens_ref, small_ref = refs[15:]
    heads, tok, _ = ds_ref.shape
    window, lanes = onehot_ref.shape
    grad = project_back(gq_ref[...], weight_halves(place_ref, 0, qk_pieces))
    grad = grad + project_back(gk_ref[...], weight_halves(place_ref, 1, qk_pieces))
    grad = grad + project_back(gv_ref[...], weight_halves(place_ref, 0, vo_pieces))
    grad = grad.T
    values = tokens_ref[...].astype(F32)
    factor = lax.rsqrt(jnp.mean(values * values, axis=-1, keepdims=True) + EPSILON)
    scaled = grad * gain_ref[...]
    inner = jnp.mean(scaled * values, axis=-1, keepdims=True)
    grad_tokens_ref[...] = grad_res_ref[...] + factor * scaled - values * (factor * factor * factor) * inner
    experts = small_ref.shape[0] - 2 - heads
    small_ref[0:1, :] = jnp.sum(grad * values * factor, axis=0, keepdims=True)
    small_ref[1:2, :] = gain_two_ref[...]
    router = mm(turn_a_ref[...], logits_a_ref[...]) + mm(turn_b_ref[...], logits_b_ref[...])
    small_ref[2 : 2 + experts, :] = router.T[:experts]
    small_ref[2 + experts :, :] = jnp.zeros((heads, small_ref.shape[1]), F32)
    row = lax.broadcasted_iota(jnp.int32, (tok, tok), 0)
    column = lax.broadcasted_iota(jnp.int32, (tok, tok), 1)
    turned = (row + column == tok - 1).astype(BF16)
    for head in range(heads):
        flipped = mm(turned, ds_ref[head])
        wide = jnp.concatenate([flipped, jnp.zeros((tok, window - tok), F32)], axis=1)
        rolled = pltpu.roll(wide, window - tok + 1, 1, stride=1, stride_axis=0)
        diagonal = jnp.broadcast_to(jnp.sum(rolled, axis=0, keepdims=True), (8, window))
        table = jnp.dot(diagonal, onehot_ref[...], precision=lax.Precision.HIGHEST, preferred_element_type=F32)
        small_ref[2 + experts + head : 3 + experts + head, 0:lanes] = table[0:1]


def second_shared_kernel(place_ref, *refs):
    pieces, out = refs[:4], refs[4]
    rows, columns = pieces[0].shape
    for target in range(4):
        x, core = target // 2, target % 2
        out[0, core * rows : (core + 1) * rows, x * columns : (x + 1) * columns] = choose(place_ref, target, pieces).astype(F32)


def first_shared_kernel(place_ref, *refs):
    pieces, out = refs[:4], refs[4]
    columns = pieces[0].shape[1]
    for target in range(4):
        out[0, :, target * columns : (target + 1) * columns] = choose(place_ref, target, pieces).astype(F32)


def attention_shared_kernel(place_ref, *refs):
    for target in range(4):
        refs[4 + target][...] = choose(place_ref, target, refs[:4]).astype(F32)


def spread(values, *others):
    far = rep_swap(values, 2)
    if others:
        far = after(far, *others)
    return [values, rep_swap(values, 1), far, rep_swap(far, 1)]


def after(values, *others):
    return lax.optimization_barrier((values,) + others)[0]


def local(
    tokens,
    doc_ids,
    routes,
    cotangent,
    attn_gain,
    w_query,
    w_key,
    w_value,
    w_output,
    rel_table,
    ffn_gain,
    w_router,
    w_in,
    w_out,
):
    tok_rows, width = tokens.shape
    head_count = rel_table.shape[1]
    experts = w_router.shape[1]
    dp_count = lax.axis_size("dp")
    expert_axis = lax.axis_size("expert")
    capacity = 2 * tok_rows // expert_axis
    inner = w_in.shape[2]
    rep = lax.axis_index("rep")
    high, low = rep // 2, rep % 2
    me = lax.axis_index("expert")
    dp = lax.axis_index("dp")
    place = jnp.stack([high, low, dp, me]).astype(jnp.int32)
    shard_rows = w_query.shape[0]
    lanes = 128
    slots = experts * capacity

    onehot = bucket_onehot(tok_rows, rel_table.shape[0])
    diag_values = jnp.dot(onehot, rel_table, precision=lax.Precision.HIGHEST).T
    square = (head_count, tok_rows, tok_rows)
    (bias,) = whole_call(
        bias_kernel, [(square, F32)], [], [diag_values, doc_ids[None, :], doc_ids[:, None]], us=2
    )

    half = width // 2
    small = jnp.concatenate([attn_gain[None], ffn_gain[None], w_router.T], axis=0)
    small_rows = -(-(2 + experts) // 16) * 16
    small = jnp.pad(small, ((0, small_rows - 2 - experts), (0, half - shard_rows)))

    def quarter(one, two):
        return lax.dynamic_slice_in_dim(jnp.where(high == 0, one, two), low * half, half, 1)

    qk_quarter = jnp.concatenate([quarter(w_query, w_key), small], axis=0)
    vo_quarter = quarter(w_value, w_output)
    if expert_axis == 2:

        def along_dp(values):
            return jnp.stack([values] + [shift(values, "dp", step) for step in range(1, dp_count)])

        qk_own, vo_own = along_dp(qk_quarter), along_dp(vo_quarter)
        qk_own = after(qk_own, bias)
        qk_got = shift(qk_own, "expert", 1)
        vo_got = shift(vo_own, "expert", 1)
        rest_shape = (dp_count * expert_axis, small_rows, lanes)
        qk_mine, rest = whole_call(
            functools.partial(lay_rows_kernel, shard_rows),
            [((width, half), BF16), (rest_shape, BF16)],
            [place],
            [qk_own, qk_got],
            us=1,
        )
        (vo_mine,) = whole_call(
            functools.partial(lay_rows_kernel, shard_rows), [((width, half), BF16)], [place], [vo_own, vo_got], us=1
        )
    else:
        rows_all = lax.all_gather(qk_quarter, ("dp", "expert"), axis=0)
        qk_mine, rest = rows_all[:, :shard_rows].reshape(width, half), rows_all[:, shard_rows:]
        vo_mine = lax.all_gather(vo_quarter, ("dp", "expert"), axis=0, tiled=True)
    rest = jnp.moveaxis(rest[:, : 2 + experts, :shard_rows], 1, 0).reshape(2 + experts, width)
    gain_one = rest[0:1].astype(F32)
    gain_two = rest[1:2].astype(F32)
    router = jnp.pad(rest[2:].T, ((0, 0), (0, lanes - experts)))
    qk_pieces = spread(qk_mine)

    route_ids = routes[:, 0]
    direct = expert_axis == 2 and capacity == tok_rows
    if direct:
        own_mask = (routes == me).astype(F32)

        def send(values):
            return values, shift(values, "expert", 1)

        def back(one, two):
            return one, shift(two, "expert", 1)

        zero = jnp.zeros_like(cotangent)
        cot_a = jnp.where(routes == me, cotangent, zero)
        cot_b = shift(after(jnp.where(routes == me, zero, cotangent), vo_got), "expert", 1)
    else:
        own_mask = jnp.ones((tok_rows, 1), F32)
        chosen = (route_ids[:, None] == jnp.arange(experts, dtype=jnp.int32)[None, :]).astype(jnp.int32)
        slot_rank = jnp.sum(jnp.cumsum(chosen, axis=0) * chosen, axis=-1) - 1
        slot_index = route_ids * capacity + slot_rank
        place_of = (jnp.arange(slots, dtype=jnp.int32)[:, None] == slot_index[None, :]).astype(BF16)

        def send(values):
            filled = mm(place_of, values).astype(BF16)
            filled = lax.all_to_all(filled, "expert", split_axis=0, concat_axis=0, tiled=True)
            return filled[: slots // 2], filled[slots // 2 :]

        def back(one, two):
            rows = jnp.concatenate([one, two], axis=0)
            rows = lax.all_to_all(rows, "expert", split_axis=0, concat_axis=0, tiled=True)
            rows = mm_tn(place_of, rows).astype(BF16)
            return rows, rows

        cot_a, cot_b = send(cotangent)

    slot_cot = jnp.concatenate([cot_a, cot_b], axis=0)
    slot_back = mm_nt(slot_cot, w_out[0]).astype(BF16)

    flat = (tok_rows, width)
    normed_one, queries, keys, probs = whole_call(
        scores_kernel,
        [(flat, BF16)] * 3 + [(square, BF16)],
        [place],
        [tokens, gain_one, *qk_pieces, bias],
        us=4,
    )
    vo_pieces = spread(after(vo_mine, qk_pieces[2]), slot_back, normed_one)
    values, attended, residual, normed_two, gate = whole_call(
        functools.partial(attend_kernel, experts),
        [(flat, BF16), (flat, BF16), (flat, F32), (flat, BF16), ((tok_rows, 1), F32)],
        [place],
        [tokens, normed_one, gain_two, router, routes, *vo_pieces, probs],
        us=4,
    )

    rows_a, rows_b = send(normed_two)
    where_me = me[None].astype(jnp.int32)
    run = functools.partial(run_expert, experts, where_me)
    hid_a, pre_a, made_a, grad_a, turn_a, cot_turn_a, logits_a = run(
        rows_a, cot_a, router, w_in, w_out, slot_back, 0
    )
    hid_b, pre_b, made_b, grad_b, turn_b, cot_turn_b, logits_b = run(
        rows_b, cot_b, router, w_in, w_out, slot_back, 1
    )
    grad_own, grad_got = back(grad_a, grad_b)

    quarter_columns = inner // 4
    second_shape, first_shape = (dp_count, width, width // 2), (2, width, quarter_columns)
    second_send, second_own, first_send, first_own = whole_call(
        outer_kernel,
        [(second_shape, BF16)] * 2 + [(first_shape, BF16)] * 2,
        [place],
        [cot_turn_a, cot_turn_b, hid_a, hid_b, turn_a, turn_b, pre_a, pre_b],
        us=BIG,
    )
    second_in = rep_swap(after(second_send, grad_got), 1)
    first_in = rep_swap(after(first_send, grad_got), 1)

    keep_part, grad_scores, grad_q, grad_k, grad_v, grad_res, grad_gain_two, send_part = whole_call(
        attend_back_kernel,
        [((2, width, width), BF16), (square, BF16)]
        + [((width, tok_rows), BF16)] * 3
        + [(flat, F32), ((1, width), F32)]
        + [((2, width, width), BF16)],
        [place],
        [own_mask, grad_own, grad_got, residual, cotangent, gain_two, attended]
        + [*vo_pieces, queries, keys, values, probs, normed_one],
        scratch=[pltpu.VMEM(flat, BF16)] + [pltpu.VMEM((width, tok_rows), BF16)] * 3,
        us=0,
    )
    core_got = rep_swap(send_part, 1)

    *early, second_send, second_keep, first_send, first_keep = whole_call(
        core_sum_kernel,
        [((2, width // 4, width // 2), BF16)] * dp_count
        + [((dp_count, width // 4, width // 2), BF16)] * 2
        + [((dp_count, width // dp_count, quarter_columns), BF16)] * 2,
        [place],
        [after(second_own, grad_res), second_in, first_own, first_in],
        us=0,
    )

    def z_sent(blocks):
        return [blocks[0]] + [shift(blocks[step], "dp", step) for step in range(1, dp_count)]

    second_got = rep_swap(second_send, 2)
    first_got = rep_swap(after(first_send, second_got), 2)
    early_z = z_sent(early)

    wide_onehot = jnp.pad(onehot, ((0, 0), (0, lanes - onehot.shape[1])))
    grad_tokens, small = whole_call(
        finish_kernel,
        [(flat, F32), ((2 + experts + head_count, width), F32)],
        [place],
        [tokens, gain_one, *qk_pieces, *vo_pieces, grad_q, grad_k, grad_v, grad_scores]
        + [after(grad_res, early[0]), grad_gain_two, wide_onehot, turn_a, turn_b, logits_a, logits_b],
        us=BIG,
    )

    if expert_axis == 2:
        shards = dp_count * expert_axis
        count = 2 + experts
        small_rows = -(-(count + head_count) // 16) * 16
        split = jnp.swapaxes(small[:count].reshape(count, shards, shard_rows), 0, 1).astype(BF16)
        split = jnp.pad(split, ((0, 0), (0, 0), (0, width - shard_rows)))
        table = jnp.broadcast_to(small[count:].astype(BF16)[None], (shards, head_count, width))
        small = jnp.concatenate([split, table], axis=1)
        small = jnp.pad(small, ((0, 0), (0, small_rows - count - head_count), (0, 0)))
        cross = (2, dp_count, shard_rows + small_rows, width)
        y_send, y_keep = whole_call(
            core_add_kernel, [(cross, BF16)] * 2, [place], [keep_part, core_got, small, rep_swap(small, 1)], us=0
        )
        y_got = shift(y_send, "expert", 1)
        token = y_send
    else:
        part = add_pair(after(keep_part, grad_tokens), core_got)
        part = part.reshape(2, dp_count, expert_axis, shard_rows, width)
        part = sum_over(part, "expert", 2)
        token = part

    (second_blocks,) = whole_call(
        plain_add_kernel, [(second_keep.shape, BF16)], [], [after(second_keep, token), second_got], us=0
    )
    early_sum = add_arrays([after(early_z[0], second_blocks)] + early_z[1:], us=BIG)
    early_got = rep_swap(early_sum[0], 2)
    second_z = lax.all_to_all(after(second_blocks, early_sum), "dp", split_axis=0, concat_axis=0, tiled=True)
    first_z = z_sent(add_arrays([after(first_keep, early_sum), first_got], dp_count, us=BIG))
    if expert_axis == 2:
        x_send, x_keep = whole_call(
            pair_add_kernel, [(cross[1:], BF16)] * 2, [place], [after(y_keep, first_z[0]), y_got], us=0
        )
        x_got = rep_swap(x_send, 2)
        token = x_keep
    else:
        x_part = add_pair(pick(part, high, 0), rep_swap(pick(part, 1 - high, 0), 2))
        token = x_part
    made_own, made_got = back(made_a, after(made_b, token))
    half_rows, half_columns = second_z.shape[1:]
    (second_sum,) = whole_call(
        second_sum_kernel,
        [((half_columns, 2 * half_rows), BF16)],
        [],
        [after(early_sum, token), early_got, second_z],
        us=0,
    )
    second_pieces = spread(second_sum)
    if expert_axis == 2:
        (x_sum,) = whole_call(
            plain_add_kernel, [(cross[1:], BF16)], [], [after(x_keep, second_sum), x_got], us=0
        )
        attn_z = lax.all_to_all(x_sum, "dp", split_axis=0, concat_axis=0, tiled=True)
        token = x_sum
    (grad_w_out,) = whole_call(
        second_shared_kernel, [((1, inner // dp_count, width), F32)], [place], second_pieces
    )
    first_sum = add_arrays([after(first_z[0], token, made_got)] + first_z[1:], us=0)
    first_pieces = spread(first_sum)
    if expert_axis == 2:
        (attn_sum,) = whole_call(
            sum_kernel, [(cross[2:], BF16)], [], [after(attn_z, first_sum)], us=0
        )
        attn_pieces = spread(attn_sum[:shard_rows])
        small = attn_sum[shard_rows:].astype(F32)
        table_total = small[2 + experts : 2 + experts + head_count, : rel_table.shape[0]].T
        small = small[: 2 + experts, :shard_rows]
    else:
        attn_pieces = spread(sum_over(x_part, "dp", 0))
        small = lax.psum(small, ("rep", "dp", "expert"))
        table_total = small[2 + experts :, : rel_table.shape[0]].T
        row_start = (dp * expert_axis + me) * shard_rows
        small = lax.dynamic_slice_in_dim(small[: 2 + experts], row_start, shard_rows, 1)
    (grad_w_in,) = whole_call(first_shared_kernel, [((1, width // dp_count, inner), F32)], [place], first_pieces)
    owned = whole_call(attention_shared_kernel, [((shard_rows, width), F32)] * 4, [place], attn_pieces)

    expert_rows = jnp.where(own_mask > 0, made_own, made_got).astype(F32)
    mixed = (residual + gate * expert_rows).astype(BF16)
    return (
        mixed,
        grad_tokens,
        small[0],
        owned[0],
        owned[1],
        owned[2],
        owned[3],
        table_total,
        small[1],
        small[2:].T,
        grad_w_in,
        grad_w_out,
    )


def solution(mesh):
    rows = P(("rep", "dp", "expert"), None)
    split = P(("dp", "expert"), None)
    vector = P(("dp", "expert"))
    return jax.shard_map(
        local,
        mesh=mesh,
        in_specs=(
            rows,
            P(("rep", "dp", "expert")),
            rows,
            rows,
            vector,
            split,
            split,
            split,
            split,
            P(),
            vector,
            split,
            P("expert", None, None),
            P("expert", None, None),
        ),
        out_specs=(
            rows,
            rows,
            vector,
            split,
            split,
            split,
            split,
            P(),
            vector,
            split,
            P("expert", "dp", None),
            P("expert", "dp", None),
        ),
        check_vma=False,
    )
```

```python
import functools

import jax
import jax.numpy as jnp
from jax import lax
from jax.experimental import pallas as pl
from jax.experimental.pallas import tpu as pltpu
from jax.sharding import PartitionSpec as P

EPSILON = 1e-06
BUCKET_BOUNDS = (12, 16, 23, 32, 46, 64, 91)
INV_ROOT_TWO = 0.7071067811865476
INV_ROOT_TWO_PI = 0.3989422804014327
BF16 = jnp.bfloat16
F32 = jnp.float32


def bucket_of(offsets):
    distance = jnp.abs(offsets)
    levels = jnp.minimum(distance, 8)
    for threshold in BUCKET_BOUNDS:
        levels = levels + (distance >= threshold).astype(jnp.int32)
    return levels + 16 * (offsets > 0).astype(jnp.int32)


def bucket_onehot(tok_rows, bucket_count):
    window = 2 * tok_rows
    places = jnp.arange(window, dtype=jnp.int32)
    offsets = jnp.where(places < tok_rows, places, places - window)
    return (
        bucket_of(offsets)[:, None] == jnp.arange(bucket_count, dtype=jnp.int32)[None, :]
    ).astype(F32)


def rep_swap(values, bit):
    count = lax.axis_size("rep")
    return lax.ppermute(values, "rep", [(i, i ^ bit) for i in range(count)])


def shift(values, axis, step):
    count = lax.axis_size(axis)
    return lax.ppermute(values, axis, [(i, (i + step) % count) for i in range(count)])


def pick(values, index, axis):
    return lax.dynamic_index_in_dim(values, index, axis, keepdims=False)


def add_pair(one, two):
    return (one.astype(F32) + two.astype(F32)).astype(BF16)


def sum_over(values, axis, dimension):
    total = lax.psum_scatter(values.astype(F32), axis, scatter_dimension=dimension, tiled=False)
    return total.astype(BF16)


VMEM_BYTES = 26 * 1024 * 1024
EXPERT_VMEM = 18 * 1024 * 1024
BIG = 30
NT = (((1,), (1,)), ((), ()))
TN = (((0,), (0,)), ((), ()))


def mm(one, two):
    return jnp.dot(one, two, preferred_element_type=F32)


def mm_nt(one, two):
    return lax.dot_general(one, two, NT, preferred_element_type=F32)


def mm_tn(one, two):
    return lax.dot_general(one, two, TN, preferred_element_type=F32)


def estimate(us):
    return pl.CostEstimate(flops=us * 10**9 + 1, bytes_accessed=us * 10**6 + 1, transcendentals=0)


def whole_call(kernel, outs, scalars, arrays, scratch=(), us=2, vmem_bytes=VMEM_BYTES):
    vmem = pl.BlockSpec(memory_space=pltpu.VMEM)
    return pl.pallas_call(
        kernel,
        out_shape=[jax.ShapeDtypeStruct(s, d) for s, d in outs],
        in_specs=[pl.BlockSpec(memory_space=pltpu.SMEM)] * len(scalars) + [vmem] * len(arrays),
        out_specs=[vmem] * len(outs),
        scratch_shapes=list(scratch),
        cost_estimate=estimate(us),
        compiler_params=pltpu.CompilerParams(vmem_limit_bytes=vmem_bytes),
    )(*scalars, *arrays)


def bias_kernel(diag_ref, row_ref, col_ref, bias_ref):
    heads, tok, _ = bias_ref.shape
    window = diag_ref.shape[1]
    same = row_ref[...] == col_ref[...]
    for head in range(heads):
        wide = jnp.broadcast_to(diag_ref[head : head + 1, :], (tok, window))
        rolled = pltpu.roll(wide, 0, 1, stride=1, stride_axis=0)
        bias_ref[head] = jnp.where(same, rolled[:, :tok], -1e30)


def choose(place_ref, target, pieces):
    at = jnp.bitwise_xor(2 * place_ref[0] + place_ref[1], target)
    near = jnp.where(at % 2 == 0, pieces[0][...], pieces[1][...])
    far = jnp.where(at % 2 == 0, pieces[2][...], pieces[3][...])
    return jnp.where(at < 2, near, far)


def weight_halves(place_ref, index, pieces):
    return choose(place_ref, 2 * index, pieces), choose(place_ref, 2 * index + 1, pieces)


def project(values, halves):
    return jnp.concatenate([mm(values, halves[0]), mm(values, halves[1])], axis=1)


def project_back(turned, halves):
    half = turned.shape[0] // 2
    return mm(halves[0], turned[:half]) + mm(halves[1], turned[half:])


def low_lanes(tok, head_size):
    return lax.broadcasted_iota(jnp.int32, (tok, 2 * head_size), 1) < head_size


def scores_kernel(place_ref, tokens_ref, gain_ref, *refs):
    pieces = refs[:4]
    bias_ref, normed_ref, q_ref, k_ref, probs_ref = refs[4:]
    heads, tok, _ = bias_ref.shape
    size = tokens_ref.shape[1] // heads
    values = tokens_ref[...].astype(F32)
    factor = lax.rsqrt(jnp.mean(values * values, axis=-1, keepdims=True) + EPSILON)
    normed = (values * factor * gain_ref[...]).astype(BF16)
    normed_ref[...] = normed
    q_ref[...] = project(normed, weight_halves(place_ref, 0, pieces)).astype(BF16)
    k_ref[...] = project(normed, weight_halves(place_ref, 1, pieces)).astype(BF16)
    first = low_lanes(tok, size)
    for pair in range(heads // 2):
        lanes = slice(pair * 2 * size, (pair + 1) * 2 * size)
        queries, keys = q_ref[:, lanes], k_ref[:, lanes]
        for part in range(2):
            head = 2 * pair + part
            picked = jnp.where(first if part == 0 else ~first, queries, jnp.zeros_like(queries))
            scores = mm_nt(picked, keys) + bias_ref[head]
            exponent = jnp.exp(scores - jnp.max(scores, axis=-1, keepdims=True))
            probs = exponent / jnp.sum(exponent, axis=-1, keepdims=True)
            probs_ref[head] = probs.astype(BF16)


def attend_kernel(
    experts,
    place_ref,
    tokens_ref,
    normed_ref,
    gain_ref,
    router_ref,
    routes_ref,
    *refs,
):
    pieces = refs[:4]
    probs_ref, v_ref, attended_ref, residual_ref, normed_two_ref, gate_ref = refs[4:]
    heads, tok, _ = probs_ref.shape
    size = tokens_ref.shape[1] // heads
    v_ref[...] = project(normed_ref[...], weight_halves(place_ref, 0, pieces)).astype(BF16)
    first = low_lanes(tok, size)
    for pair in range(heads // 2):
        lanes = slice(pair * 2 * size, (pair + 1) * 2 * size)
        made = [mm(probs_ref[2 * pair + part], v_ref[:, lanes]) for part in range(2)]
        attended_ref[:, lanes] = jnp.where(first, made[0], made[1]).astype(BF16)
    halves = weight_halves(place_ref, 1, pieces)
    residual = tokens_ref[...].astype(F32) + project(attended_ref[...], halves)
    residual_ref[...] = residual
    factor = lax.rsqrt(jnp.mean(residual * residual, axis=-1, keepdims=True) + EPSILON)
    normed = (residual * factor * gain_ref[...]).astype(BF16)
    normed_two_ref[...] = normed
    probs = router_softmax(normed, router_ref[...], experts)
    lane = lax.broadcasted_iota(jnp.int32, probs.shape, 1)
    gate_ref[...] = jnp.sum(jnp.where(lane == routes_ref[...], probs, 0.0), axis=-1, keepdims=True)


def router_softmax(normed, router, experts):
    logits = mm(normed, router)
    lane = lax.broadcasted_iota(jnp.int32, logits.shape, 1)
    logits = jnp.where(lane < experts, logits, -1e30)
    exponent = jnp.exp(logits - jnp.max(logits, axis=-1, keepdims=True))
    return exponent / jnp.sum(exponent, axis=-1, keepdims=True)


def expert_kernel(
    experts,
    me_ref,
    rows_ref,
    cot_ref,
    router_ref,
    first_ref,
    second_ref,
    back_ref,
    hidden_ref,
    grad_pre_ref,
    produced_ref,
    grad_rows_ref,
    rows_turned_ref,
    cot_turned_ref,
    grad_logits_ref,
    made_ref,
    grad_ref,
    probs_ref,
):
    step, steps = pl.program_id(0), pl.num_programs(0)

    @pl.when(step == 0)
    def _():
        probs_ref[...] = router_softmax(rows_ref[...], router_ref[...], experts)
        rows_turned_ref[...] = rows_ref[...].T

    probs = probs_ref[...]
    chosen = lax.broadcasted_iota(jnp.int32, probs.shape, 1) == me_ref[0]
    gate = jnp.sum(jnp.where(chosen, probs, 0.0), axis=-1, keepdims=True)
    pre_act = mm(rows_ref[...], first_ref[0])
    cdf = 0.5 + 0.5 * lax.erf(pre_act * INV_ROOT_TWO)
    hidden = (pre_act * cdf).astype(BF16)
    slope = cdf + pre_act * jnp.exp(-0.5 * pre_act * pre_act) * INV_ROOT_TWO_PI
    grad_pre = (back_ref[...].astype(F32) * gate * slope).astype(BF16)
    hidden_ref[...] = hidden
    grad_pre_ref[...] = grad_pre
    made = mm(hidden, second_ref[0])
    grad = mm_nt(grad_pre, first_ref[0])

    @pl.when(step == 0)
    def _():
        made_ref[...] = made
        grad_ref[...] = grad

    @pl.when(step > 0)
    def _():
        made_ref[...] += made
        grad_ref[...] += grad

    @pl.when(step == steps - 1)
    def _():
        produced = made_ref[...].astype(BF16)
        produced_ref[...] = produced
        cot = cot_ref[...].astype(F32)
        grad_gate = jnp.sum(cot * produced.astype(F32), axis=-1, keepdims=True)
        grad_logits = (grad_gate * gate * (chosen.astype(F32) - probs)).astype(BF16)
        grad_logits_ref[...] = grad_logits
        grad_rows_ref[...] = (grad_ref[...] + mm_nt(grad_logits, router_ref[...])).astype(BF16)
        cot_turned_ref[...] = (cot * gate).astype(BF16).T


def run_expert(experts, me, rows, cot, router, w_in, w_out, slot_back, part):
    count, width = rows.shape
    inner = w_in.shape[2]
    tile = 1024
    lanes = router.shape[1]
    const = lambda shape: pl.BlockSpec(shape, lambda j, s: (0, 0))
    wide = pl.BlockSpec((count, tile), lambda j, s: (0, j))
    return pl.pallas_call(
        functools.partial(expert_kernel, experts),
        out_shape=[
            jax.ShapeDtypeStruct((count, inner), BF16),
            jax.ShapeDtypeStruct((count, inner), BF16),
            jax.ShapeDtypeStruct((count, width), BF16),
            jax.ShapeDtypeStruct((count, width), BF16),
            jax.ShapeDtypeStruct((width, count), BF16),
            jax.ShapeDtypeStruct((width, count), BF16),
            jax.ShapeDtypeStruct((count, lanes), BF16),
        ],
        grid_spec=pltpu.PrefetchScalarGridSpec(
            num_scalar_prefetch=1,
            grid=(inner // tile,),
            in_specs=[
                const((count, width)),
                const((count, width)),
                const((width, lanes)),
                pl.BlockSpec((1, width, tile), lambda j, s: (0, 0, j)),
                pl.BlockSpec((1, tile, width), lambda j, s: (0, j, 0)),
                pl.BlockSpec((count, tile), lambda j, s: (part, j)),
            ],
            out_specs=[wide, wide]
            + [const((count, width))] * 2
            + [const((width, count))] * 2
            + [const((count, lanes))],
            scratch_shapes=[
                pltpu.VMEM((count, width), F32),
                pltpu.VMEM((count, width), F32),
                pltpu.VMEM((count, lanes), F32),
            ],
        ),
        cost_estimate=estimate(9),
        compiler_params=pltpu.CompilerParams(vmem_limit_bytes=EXPERT_VMEM),
    )(me, rows, cot, router, w_in, w_out, slot_back)


def outer_kernel(place_ref, *refs):
    cots, hidden, rows, grad_pre = refs[0:2], refs[2:4], refs[4:6], refs[6:8]
    second_send, second_own, first_send, first_own = refs[8:]
    high, low, dp = place_ref[0], place_ref[1], place_ref[2]
    blocks, _, columns = second_send.shape
    for block in range(blocks):
        for core, out in ((1 - low, second_send), (low, second_own)):
            start = (2 * lax.rem(block + dp, blocks) + core) * columns
            lanes = pl.ds(pl.multiple_of(start, 128), columns)
            out[block] = (mm(cots[0][...], hidden[0][:, lanes]) + mm(cots[1][...], hidden[1][:, lanes])).astype(BF16)
    columns = first_send.shape[2]
    for index, x in enumerate((1 - high, high)):
        for core, out in ((1 - low, first_send), (low, first_own)):
            lanes = pl.ds(pl.multiple_of((2 * x + core) * columns, 128), columns)
            out[index] = (mm(rows[0][...], grad_pre[0][:, lanes]) + mm(rows[1][...], grad_pre[1][:, lanes])).astype(BF16)


def core_sum_kernel(place_ref, second_own, second_got, first_own, first_got, *outs):
    high, dp = place_ref[0], place_ref[2]
    blocks, width, _ = second_own.shape
    half, rows = width // 2, width // 4
    for block in range(blocks):
        total = (second_own[block].astype(F32) + second_got[block].astype(F32)).astype(BF16)
        send = jnp.where(high == 0, total[half:], total[:half])
        kept = jnp.where(high == 0, total[:half], total[half:])
        outs[block][0] = send[:rows]
        outs[block][1] = kept[:rows]
        at = lax.rem(block + dp, blocks)
        outs[blocks][at] = send[rows:]
        outs[blocks + 1][at] = kept[rows:]
    rows = width // blocks
    for index in range(2):
        for block in range(blocks):
            lines = slice(block * rows, (block + 1) * rows)
            total = first_own[index, lines].astype(F32) + first_got[index, lines].astype(F32)
            outs[blocks + 2 + index][lax.rem(block - dp + blocks, blocks)] = total.astype(BF16)


def add_kernel(count, *refs):
    ins, outs = refs[: len(refs) - count], refs[len(refs) - count :]
    for index, out in enumerate(outs):
        total = 0.0
        for ref in ins:
            total = total + (ref[index] if count > 1 else ref[...]).astype(F32)
        out[...] = total.astype(BF16)


def add_arrays(arrays, count=1, us=BIG):
    shape = arrays[0].shape[1:] if count > 1 else arrays[0].shape
    outs = whole_call(functools.partial(add_kernel, count), [(shape, BF16)] * count, [], arrays, us=us)
    return outs if count > 1 else outs[0]


def core_add_kernel(place_ref, keep_ref, got_ref, send_ref, mine_ref):
    blocks, rows = send_ref.shape[1], send_ref.shape[2]
    me = place_ref[3]
    for matrix in range(2):
        for block in range(blocks):
            start = 2 * block * rows
            total = keep_ref[matrix, start : start + 2 * rows].astype(F32)
            total = (total + got_ref[matrix, start : start + 2 * rows].astype(F32)).astype(BF16)
            one, two = total[:rows], total[rows:]
            mine_ref[matrix, block] = jnp.where(me == 0, one, two)
            send_ref[matrix, block] = jnp.where(me == 0, two, one)


def pair_add_kernel(place_ref, keep_ref, got_ref, small_keep_ref, small_got_ref, send_ref, mine_ref):
    high = place_ref[0]
    rows = keep_ref.shape[2]
    send_ref[:, :rows] = (keep_ref[1 - high].astype(F32) + got_ref[1 - high].astype(F32)).astype(BF16)
    mine_ref[:, :rows] = (keep_ref[high].astype(F32) + got_ref[high].astype(F32)).astype(BF16)
    small = (small_keep_ref[...].astype(F32) + small_got_ref[...].astype(F32)).astype(BF16)
    send_ref[:, rows:] = small
    mine_ref[:, rows:] = small


def plain_add_kernel(one, two, out):
    out[...] = (one[...].astype(F32) + two[...].astype(F32)).astype(BF16)


def sum_kernel(blocks, out):
    total = blocks[0].astype(F32)
    for block in range(1, blocks.shape[0]):
        total = total + blocks[block].astype(F32)
    out[...] = total.astype(BF16)


def second_sum_kernel(early_keep, early_got, blocks, out):
    low = blocks[0].astype(F32)
    for block in range(1, blocks.shape[0]):
        low = low + blocks[block].astype(F32)
    high = early_keep[1].astype(F32) + early_got[...].astype(F32)
    out[...] = jnp.concatenate([high, low], axis=0).T.astype(BF16)


def lay_rows_kernel(rows, place_ref, own_ref, got_ref, out_ref, *rest):
    blocks = own_ref.shape[0]
    me = place_ref[3]
    for block in range(blocks):
        at = lax.rem(place_ref[2] - block + blocks, blocks)
        own, got = own_ref[at], got_ref[at]
        both = (jnp.where(me == 0, own, got), jnp.where(me == 0, got, own))
        for index in range(2):
            start = (2 * block + index) * rows
            out_ref[start : start + rows, :] = both[index][:rows]
            for ref in rest:
                ref[2 * block + index] = both[index][rows:, : ref.shape[2]]


def attend_back_kernel(
    place_ref,
    mask_ref,
    own_ref,
    got_ref,
    residual_ref,
    cot_ref,
    gain_ref,
    attended_ref,
    *refs,
):
    pieces = refs[:4]
    q_ref, k_ref, v_ref, probs_ref, normed_ref, keep_ref, ds_ref, gq_ref, gk_ref, gv_ref = refs[4:14]
    grad_res_ref, gain_grad_ref, send_ref, ga_ref, gat_ref, qt_ref, kt_ref = refs[14:]
    heads, tok, _ = probs_ref.shape
    size = residual_ref.shape[1] // heads
    low = place_ref[1]

    def store(index, grad):
        grad = grad.astype(BF16)

        @pl.when(low == index % 2)
        def _():
            keep_ref[index // 2] = grad

        @pl.when(low != index % 2)
        def _():
            send_ref[index // 2] = grad

    grad_two = jnp.where(mask_ref[...] > 0, own_ref[...], got_ref[...]).astype(F32)
    residual = residual_ref[...]
    factor = lax.rsqrt(jnp.mean(residual * residual, axis=-1, keepdims=True) + EPSILON)
    scaled = grad_two * gain_ref[...]
    inner = jnp.mean(scaled * residual, axis=-1, keepdims=True)
    grad_res = cot_ref[...].astype(F32) + factor * scaled - residual * (factor * factor * factor) * inner
    grad_res_ref[...] = grad_res
    gain_grad_ref[...] = jnp.sum(grad_two * residual * factor, axis=0, keepdims=True)
    grad_attn = grad_res.astype(BF16)
    store(3, mm(attended_ref[...].T, grad_attn))
    left, right = weight_halves(place_ref, 1, pieces)
    half = left.shape[1]
    ga_ref[...] = (mm_nt(grad_attn[:, :half], left) + mm_nt(grad_attn[:, half:], right)).astype(BF16)
    gat_ref[...] = (mm_nt(left, grad_attn[:, :half]) + mm_nt(right, grad_attn[:, half:])).astype(BF16)
    qt_ref[...] = q_ref[...].T
    kt_ref[...] = k_ref[...].T
    first = low_lanes(tok, size)
    for head in range(heads):
        lanes = slice(head // 2 * 2 * size, (head // 2 + 1) * 2 * size)
        rows = slice(head * size, (head + 1) * size)
        grads = ga_ref[:, lanes]
        picked = jnp.where(first if head % 2 == 0 else ~first, grads, jnp.zeros_like(grads))
        grad_probs = mm_nt(picked, v_ref[:, lanes])
        probs = probs_ref[head]
        wide = probs.astype(F32)
        total = jnp.sum(wide * grad_probs, axis=-1, keepdims=True)
        ds = (wide * (grad_probs - total)).astype(BF16)
        ds_ref[head] = ds
        gq_ref[rows, :] = mm_nt(kt_ref[rows, :], ds).astype(BF16)
        gk_ref[rows, :] = mm(qt_ref[rows, :], ds).astype(BF16)
        gv_ref[rows, :] = mm(gat_ref[rows, :], probs).astype(BF16)
    turned = normed_ref[...].T
    store(0, mm_nt(turned, gq_ref[...]))
    store(1, mm_nt(turned, gk_ref[...]))
    store(2, mm_nt(turned, gv_ref[...]))


def finish_kernel(
    place_ref,
    tokens_ref,
    gain_ref,
    *refs,
):
    qk_pieces, vo_pieces = refs[:4], refs[4:8]
    gq_ref, gk_ref, gv_ref, ds_ref, grad_res_ref, gain_two_ref, onehot_ref = refs[8:15]
    turn_a_ref, turn_b_ref, logits_a_ref, logits_b_ref, grad_tokens_ref, small_ref = refs[15:]
    heads, tok, _ = ds_ref.shape
    window, lanes = onehot_ref.shape
    grad = project_back(gq_ref[...], weight_halves(place_ref, 0, qk_pieces))
    grad = grad + project_back(gk_ref[...], weight_halves(place_ref, 1, qk_pieces))
    grad = grad + project_back(gv_ref[...], weight_halves(place_ref, 0, vo_pieces))
    grad = grad.T
    values = tokens_ref[...].astype(F32)
    factor = lax.rsqrt(jnp.mean(values * values, axis=-1, keepdims=True) + EPSILON)
    scaled = grad * gain_ref[...]
    inner = jnp.mean(scaled * values, axis=-1, keepdims=True)
    grad_tokens_ref[...] = grad_res_ref[...] + factor * scaled - values * (factor * factor * factor) * inner
    experts = small_ref.shape[0] - 2 - heads
    small_ref[0:1, :] = jnp.sum(grad * values * factor, axis=0, keepdims=True)
    small_ref[1:2, :] = gain_two_ref[...]
    router = mm(turn_a_ref[...], logits_a_ref[...]) + mm(turn_b_ref[...], logits_b_ref[...])
    small_ref[2 : 2 + experts, :] = router.T[:experts]
    small_ref[2 + experts :, :] = jnp.zeros((heads, small_ref.shape[1]), F32)
    row = lax.broadcasted_iota(jnp.int32, (tok, tok), 0)
    column = lax.broadcasted_iota(jnp.int32, (tok, tok), 1)
    turned = (row + column == tok - 1).astype(BF16)
    for head in range(heads):
        flipped = mm(turned, ds_ref[head])
        wide = jnp.concatenate([flipped, jnp.zeros((tok, window - tok), F32)], axis=1)
        rolled = pltpu.roll(wide, window - tok + 1, 1, stride=1, stride_axis=0)
        diagonal = jnp.broadcast_to(jnp.sum(rolled, axis=0, keepdims=True), (8, window))
        table = jnp.dot(diagonal, onehot_ref[...], precision=lax.Precision.HIGHEST, preferred_element_type=F32)
        small_ref[2 + experts + head : 3 + experts + head, 0:lanes] = table[0:1]


def second_shared_kernel(place_ref, *refs):
    pieces, out = refs[:4], refs[4]
    rows, columns = pieces[0].shape
    for target in range(4):
        x, core = target // 2, target % 2
        out[0, core * rows : (core + 1) * rows, x * columns : (x + 1) * columns] = choose(place_ref, target, pieces).astype(F32)


def first_shared_kernel(place_ref, *refs):
    pieces, out = refs[:4], refs[4]
    columns = pieces[0].shape[1]
    for target in range(4):
        out[0, :, target * columns : (target + 1) * columns] = choose(place_ref, target, pieces).astype(F32)


def attention_shared_kernel(place_ref, *refs):
    for target in range(4):
        refs[4 + target][...] = choose(place_ref, target, refs[:4]).astype(F32)


def spread(values, *others):
    far = rep_swap(values, 2)
    if others:
        far = after(far, *others)
    return [values, rep_swap(values, 1), far, rep_swap(far, 1)]


def after(values, *others):
    return lax.optimization_barrier((values,) + others)[0]


def local(
    tokens,
    doc_ids,
    routes,
    cotangent,
    attn_gain,
    w_query,
    w_key,
    w_value,
    w_output,
    rel_table,
    ffn_gain,
    w_router,
    w_in,
    w_out,
):
    tok_rows, width = tokens.shape
    head_count = rel_table.shape[1]
    experts = w_router.shape[1]
    dp_count = lax.axis_size("dp")
    expert_axis = lax.axis_size("expert")
    capacity = 2 * tok_rows // expert_axis
    inner = w_in.shape[2]
    rep = lax.axis_index("rep")
    high, low = rep // 2, rep % 2
    me = lax.axis_index("expert")
    dp = lax.axis_index("dp")
    place = jnp.stack([high, low, dp, me]).astype(jnp.int32)
    shard_rows = w_query.shape[0]
    lanes = 128
    slots = experts * capacity

    onehot = bucket_onehot(tok_rows, rel_table.shape[0])
    diag_values = jnp.dot(onehot, rel_table, precision=lax.Precision.HIGHEST).T
    square = (head_count, tok_rows, tok_rows)
    (bias,) = whole_call(
        bias_kernel, [(square, F32)], [], [diag_values, doc_ids[None, :], doc_ids[:, None]], us=2
    )

    half = width // 2
    small = jnp.concatenate([attn_gain[None], ffn_gain[None], w_router.T], axis=0)
    small_rows = -(-(2 + experts) // 16) * 16
    small = jnp.pad(small, ((0, small_rows - 2 - experts), (0, half - shard_rows)))

    def quarter(one, two):
        return lax.dynamic_slice_in_dim(jnp.where(high == 0, one, two), low * half, half, 1)

    qk_quarter = jnp.concatenate([quarter(w_query, w_key), small], axis=0)
    vo_quarter = quarter(w_value, w_output)
    if expert_axis == 2:

        def along_dp(values):
            return jnp.stack([values] + [shift(values, "dp", step) for step in range(1, dp_count)])

        qk_own, vo_own = along_dp(qk_quarter), along_dp(vo_quarter)
        qk_own = after(qk_own, bias)
        qk_got = shift(qk_own, "expert", 1)
        vo_got = shift(vo_own, "expert", 1)
        rest_shape = (dp_count * expert_axis, small_rows, lanes)
        qk_mine, rest = whole_call(
            functools.partial(lay_rows_kernel, shard_rows),
            [((width, half), BF16), (rest_shape, BF16)],
            [place],
            [qk_own, qk_got],
            us=1,
        )
        (vo_mine,) = whole_call(
            functools.partial(lay_rows_kernel, shard_rows), [((width, half), BF16)], [place], [vo_own, vo_got], us=1
        )
    else:
        rows_all = lax.all_gather(qk_quarter, ("dp", "expert"), axis=0)
        qk_mine, rest = rows_all[:, :shard_rows].reshape(width, half), rows_all[:, shard_rows:]
        vo_mine = lax.all_gather(vo_quarter, ("dp", "expert"), axis=0, tiled=True)
    rest = jnp.moveaxis(rest[:, : 2 + experts, :shard_rows], 1, 0).reshape(2 + experts, width)
    gain_one = rest[0:1].astype(F32)
    gain_two = rest[1:2].astype(F32)
    router = jnp.pad(rest[2:].T, ((0, 0), (0, lanes - experts)))
    qk_pieces = spread(qk_mine)

    route_ids = routes[:, 0]
    direct = expert_axis == 2 and capacity == tok_rows
    if direct:
        own_mask = (routes == me).astype(F32)

        def send(values):
            return values, shift(values, "expert", 1)

        def back(one, two):
            return one, shift(two, "expert", 1)

        zero = jnp.zeros_like(cotangent)
        cot_a = jnp.where(routes == me, cotangent, zero)
        cot_b = shift(after(jnp.where(routes == me, zero, cotangent), vo_got), "expert", 1)
    else:
        own_mask = jnp.ones((tok_rows, 1), F32)
        chosen = (route_ids[:, None] == jnp.arange(experts, dtype=jnp.int32)[None, :]).astype(jnp.int32)
        slot_rank = jnp.sum(jnp.cumsum(chosen, axis=0) * chosen, axis=-1) - 1
        slot_index = route_ids * capacity + slot_rank
        place_of = (jnp.arange(slots, dtype=jnp.int32)[:, None] == slot_index[None, :]).astype(BF16)

        def send(values):
            filled = mm(place_of, values).astype(BF16)
            filled = lax.all_to_all(filled, "expert", split_axis=0, concat_axis=0, tiled=True)
            return filled[: slots // 2], filled[slots // 2 :]

        def back(one, two):
            rows = jnp.concatenate([one, two], axis=0)
            rows = lax.all_to_all(rows, "expert", split_axis=0, concat_axis=0, tiled=True)
            rows = mm_tn(place_of, rows).astype(BF16)
            return rows, rows

        cot_a, cot_b = send(cotangent)

    slot_cot = jnp.concatenate([cot_a, cot_b], axis=0)
    slot_back = mm_nt(slot_cot, w_out[0]).astype(BF16)

    flat = (tok_rows, width)
    normed_one, queries, keys, probs = whole_call(
        scores_kernel,
        [(flat, BF16)] * 3 + [(square, BF16)],
        [place],
        [tokens, gain_one, *qk_pieces, bias],
        us=4,
    )
    vo_pieces = spread(after(vo_mine, qk_pieces[2]), slot_back, normed_one)
    values, attended, residual, normed_two, gate = whole_call(
        functools.partial(attend_kernel, experts),
        [(flat, BF16), (flat, BF16), (flat, F32), (flat, BF16), ((tok_rows, 1), F32)],
        [place],
        [tokens, normed_one, gain_two, router, routes, *vo_pieces, probs],
        us=4,
    )

    rows_a, rows_b = send(normed_two)
    where_me = me[None].astype(jnp.int32)
    run = functools.partial(run_expert, experts, where_me)
    hid_a, pre_a, made_a, grad_a, turn_a, cot_turn_a, logits_a = run(
        rows_a, cot_a, router, w_in, w_out, slot_back, 0
    )
    hid_b, pre_b, made_b, grad_b, turn_b, cot_turn_b, logits_b = run(
        rows_b, cot_b, router, w_in, w_out, slot_back, 1
    )
    grad_own, grad_got = back(grad_a, grad_b)

    quarter_columns = inner // 4
    second_shape, first_shape = (dp_count, width, width // 2), (2, width, quarter_columns)
    second_send, second_own, first_send, first_own = whole_call(
        outer_kernel,
        [(second_shape, BF16)] * 2 + [(first_shape, BF16)] * 2,
        [place],
        [cot_turn_a, cot_turn_b, hid_a, hid_b, turn_a, turn_b, pre_a, pre_b],
        us=BIG,
    )
    second_in = rep_swap(after(second_send, grad_got), 1)
    first_in = rep_swap(after(first_send, grad_got), 1)

    keep_part, grad_scores, grad_q, grad_k, grad_v, grad_res, grad_gain_two, send_part = whole_call(
        attend_back_kernel,
        [((2, width, width), BF16), (square, BF16)]
        + [((width, tok_rows), BF16)] * 3
        + [(flat, F32), ((1, width), F32)]
        + [((2, width, width), BF16)],
        [place],
        [own_mask, grad_own, grad_got, residual, cotangent, gain_two, attended]
        + [*vo_pieces, queries, keys, values, probs, normed_one],
        scratch=[pltpu.VMEM(flat, BF16)] + [pltpu.VMEM((width, tok_rows), BF16)] * 3,
        us=0,
    )
    core_got = rep_swap(send_part, 1)

    *early, second_send, second_keep, first_send, first_keep = whole_call(
        core_sum_kernel,
        [((2, width // 4, width // 2), BF16)] * dp_count
        + [((dp_count, width // 4, width // 2), BF16)] * 2
        + [((dp_count, width // dp_count, quarter_columns), BF16)] * 2,
        [place],
        [after(second_own, grad_res), second_in, first_own, first_in],
        us=0,
    )

    def z_sent(blocks):
        return [blocks[0]] + [shift(blocks[step], "dp", step) for step in range(1, dp_count)]

    second_got = rep_swap(second_send, 2)
    first_got = rep_swap(after(first_send, second_got), 2)
    early_z = z_sent(early)

    if expert_axis == 2:
        cross = (2, dp_count, shard_rows, width)
        y_send, y_keep = whole_call(
            core_add_kernel, [(cross, BF16)] * 2, [place], [after(keep_part, early[0]), core_got], us=BIG
        )
        y_got = shift(y_send, "expert", 1)
        token = y_send
    else:
        part = add_pair(after(keep_part, early[0]), core_got)
        part = part.reshape(2, dp_count, expert_axis, shard_rows, width)
        part = sum_over(part, "expert", 2)
        token = part

    wide_onehot = jnp.pad(onehot, ((0, 0), (0, lanes - onehot.shape[1])))
    grad_tokens, small = whole_call(
        finish_kernel,
        [(flat, F32), ((2 + experts + head_count, width), F32)],
        [place],
        [tokens, gain_one, *qk_pieces, *vo_pieces, grad_q, grad_k, grad_v, grad_scores]
        + [after(grad_res, token), grad_gain_two, wide_onehot, turn_a, turn_b, logits_a, logits_b],
        us=BIG,
    )
    (second_blocks,) = whole_call(
        plain_add_kernel, [(second_keep.shape, BF16)], [], [after(second_keep, grad_tokens), second_got], us=0
    )
    early_sum = add_arrays([after(early_z[0], second_blocks)] + early_z[1:], us=0)
    early_got = rep_swap(early_sum[0], 2)
    second_z = lax.all_to_all(after(second_blocks, early_sum), "dp", split_axis=0, concat_axis=0, tiled=True)
    if expert_axis == 2:
        shards = dp_count * expert_axis
        count = 2 + experts
        small_rows = -(-(count + head_count) // 16) * 16
        split = jnp.swapaxes(small[:count].reshape(count, shards, shard_rows), 0, 1).astype(BF16)
        split = jnp.pad(split, ((0, 0), (0, 0), (0, width - shard_rows)))
        table = jnp.broadcast_to(small[count:].astype(BF16)[None], (shards, head_count, width))
        small = jnp.concatenate([split, table], axis=1)
        small = jnp.pad(small, ((0, 0), (0, small_rows - count - head_count), (0, 0)))
        small = after(small, early_sum)
        small = add_pair(small, rep_swap(small, 1)).reshape(dp_count, 2, small_rows, width)
        small_got = shift(pick(small, 1 - me, 1), "expert", 1)
        small_keep = pick(small, me, 1)
    first_z = z_sent(add_arrays([after(first_keep, early_sum), first_got], dp_count, us=0))
    if expert_axis == 2:
        x_send, x_keep = whole_call(
            pair_add_kernel,
            [((dp_count, shard_rows + small_rows, width), BF16)] * 2,
            [place],
            [after(y_keep, first_z[0]), y_got, small_keep, small_got],
            us=0,
        )
        x_got = rep_swap(x_send, 2)
        token = x_keep
    else:
        x_part = add_pair(pick(part, high, 0), rep_swap(pick(part, 1 - high, 0), 2))
        token = x_part
    half_rows, half_columns = second_z.shape[1:]
    (second_sum,) = whole_call(
        second_sum_kernel,
        [((half_columns, 2 * half_rows), BF16)],
        [],
        [after(early_sum, token), early_got, second_z],
        us=0,
    )
    second_pieces = spread(second_sum)
    if expert_axis == 2:
        (x_sum,) = whole_call(
            plain_add_kernel, [(x_keep.shape, BF16)], [], [after(x_keep, second_sum), x_got], us=0
        )
        attn_z = lax.all_to_all(x_sum, "dp", split_axis=0, concat_axis=0, tiled=True)
        token = x_sum
    made_own, made_got = back(made_a, after(made_b, token))
    (grad_w_out,) = whole_call(
        second_shared_kernel, [((1, inner // dp_count, width), F32)], [place], second_pieces
    )
    first_sum = add_arrays([after(first_z[0], token)] + first_z[1:], us=0)
    first_pieces = spread(first_sum)
    if expert_axis == 2:
        (attn_sum,) = whole_call(
            sum_kernel, [(x_keep.shape[1:], BF16)], [], [after(attn_z, first_sum)], us=0
        )
        attn_pieces = spread(attn_sum[:shard_rows])
        small = attn_sum[shard_rows:].astype(F32)
        table_total = small[2 + experts : 2 + experts + head_count, : rel_table.shape[0]].T
        small = small[: 2 + experts, :shard_rows]
    else:
        attn_pieces = spread(sum_over(x_part, "dp", 0))
        small = lax.psum(small, ("rep", "dp", "expert"))
        table_total = small[2 + experts :, : rel_table.shape[0]].T
        row_start = (dp * expert_axis + me) * shard_rows
        small = lax.dynamic_slice_in_dim(small[: 2 + experts], row_start, shard_rows, 1)
    (grad_w_in,) = whole_call(first_shared_kernel, [((1, width // dp_count, inner), F32)], [place], first_pieces)
    owned = whole_call(attention_shared_kernel, [((shard_rows, width), F32)] * 4, [place], attn_pieces)

    expert_rows = jnp.where(own_mask > 0, made_own, made_got).astype(F32)
    mixed = (residual + gate * expert_rows).astype(BF16)
    return (
        mixed,
        grad_tokens,
        small[0],
        owned[0],
        owned[1],
        owned[2],
        owned[3],
        table_total,
        small[1],
        small[2:].T,
        grad_w_in,
        grad_w_out,
    )


def solution(mesh):
    rows = P(("rep", "dp", "expert"), None)
    split = P(("dp", "expert"), None)
    vector = P(("dp", "expert"))
    return jax.shard_map(
        local,
        mesh=mesh,
        in_specs=(
            rows,
            P(("rep", "dp", "expert")),
            rows,
            rows,
            vector,
            split,
            split,
            split,
            split,
            P(),
            vector,
            split,
            P("expert", None, None),
            P("expert", None, None),
        ),
        out_specs=(
            rows,
            rows,
            vector,
            split,
            split,
            split,
            split,
            P(),
            vector,
            split,
            P("expert", "dp", None),
            P("expert", "dp", None),
        ),
        check_vma=False,
    )
```

```python
import functools

import jax
import jax.numpy as jnp
from jax import lax
from jax.experimental import pallas as pl
from jax.experimental.pallas import tpu as pltpu
from jax.sharding import PartitionSpec as P

EPSILON = 1e-06
BUCKET_BOUNDS = (12, 16, 23, 32, 46, 64, 91)
INV_ROOT_TWO = 0.7071067811865476
INV_ROOT_TWO_PI = 0.3989422804014327
BF16 = jnp.bfloat16
F32 = jnp.float32


def bucket_of(offsets):
    distance = jnp.abs(offsets)
    levels = jnp.minimum(distance, 8)
    for threshold in BUCKET_BOUNDS:
        levels = levels + (distance >= threshold).astype(jnp.int32)
    return levels + 16 * (offsets > 0).astype(jnp.int32)


def bucket_onehot(tok_rows, bucket_count):
    window = 2 * tok_rows
    places = jnp.arange(window, dtype=jnp.int32)
    offsets = jnp.where(places < tok_rows, places, places - window)
    return (
        bucket_of(offsets)[:, None] == jnp.arange(bucket_count, dtype=jnp.int32)[None, :]
    ).astype(F32)


def rep_swap(values, bit):
    count = lax.axis_size("rep")
    return lax.ppermute(values, "rep", [(i, i ^ bit) for i in range(count)])


def shift(values, axis, step):
    count = lax.axis_size(axis)
    return lax.ppermute(values, axis, [(i, (i + step) % count) for i in range(count)])


def pick(values, index, axis):
    return lax.dynamic_index_in_dim(values, index, axis, keepdims=False)


def add_pair(one, two):
    return (one.astype(F32) + two.astype(F32)).astype(BF16)


def sum_over(values, axis, dimension):
    total = lax.psum_scatter(values.astype(F32), axis, scatter_dimension=dimension, tiled=False)
    return total.astype(BF16)


VMEM_BYTES = 26 * 1024 * 1024
EXPERT_VMEM = 26 * 1024 * 1024
BIG = 30
NT = (((1,), (1,)), ((), ()))
TN = (((0,), (0,)), ((), ()))


def mm(one, two):
    return jnp.dot(one, two, preferred_element_type=F32)


def mm_nt(one, two):
    return lax.dot_general(one, two, NT, preferred_element_type=F32)


def mm_tn(one, two):
    return lax.dot_general(one, two, TN, preferred_element_type=F32)


def estimate(us):
    return pl.CostEstimate(flops=us * 10**9 + 1, bytes_accessed=us * 10**6 + 1, transcendentals=0)


def whole_call(kernel, outs, scalars, arrays, scratch=(), us=2, vmem_bytes=VMEM_BYTES):
    vmem = pl.BlockSpec(memory_space=pltpu.VMEM)
    return pl.pallas_call(
        kernel,
        out_shape=[jax.ShapeDtypeStruct(s, d) for s, d in outs],
        in_specs=[pl.BlockSpec(memory_space=pltpu.SMEM)] * len(scalars) + [vmem] * len(arrays),
        out_specs=[vmem] * len(outs),
        scratch_shapes=list(scratch),
        cost_estimate=estimate(us),
        compiler_params=pltpu.CompilerParams(vmem_limit_bytes=vmem_bytes),
    )(*scalars, *arrays)


def bias_kernel(diag_ref, row_ref, col_ref, bias_ref):
    heads, tok, _ = bias_ref.shape
    window = diag_ref.shape[1]
    same = row_ref[...] == col_ref[...]
    for head in range(heads):
        wide = jnp.broadcast_to(diag_ref[head : head + 1, :], (tok, window))
        rolled = pltpu.roll(wide, 0, 1, stride=1, stride_axis=0)
        bias_ref[head] = jnp.where(same, rolled[:, :tok], -1e30)


def choose(place_ref, target, pieces):
    at = jnp.bitwise_xor(2 * place_ref[0] + place_ref[1], target)
    near = jnp.where(at % 2 == 0, pieces[0][...], pieces[1][...])
    far = jnp.where(at % 2 == 0, pieces[2][...], pieces[3][...])
    return jnp.where(at < 2, near, far)


def weight_halves(place_ref, index, pieces):
    return choose(place_ref, 2 * index, pieces), choose(place_ref, 2 * index + 1, pieces)


def project(values, halves):
    return jnp.concatenate([mm(values, halves[0]), mm(values, halves[1])], axis=1)


def project_back(turned, halves):
    half = turned.shape[0] // 2
    return mm(halves[0], turned[:half]) + mm(halves[1], turned[half:])


def low_lanes(tok, head_size):
    return lax.broadcasted_iota(jnp.int32, (tok, 2 * head_size), 1) < head_size


def scores_kernel(place_ref, tokens_ref, gain_ref, *refs):
    pieces = refs[:4]
    bias_ref, normed_ref, q_ref, k_ref, probs_ref = refs[4:]
    heads, tok, _ = bias_ref.shape
    size = tokens_ref.shape[1] // heads
    values = tokens_ref[...].astype(F32)
    factor = lax.rsqrt(jnp.mean(values * values, axis=-1, keepdims=True) + EPSILON)
    normed = (values * factor * gain_ref[...]).astype(BF16)
    normed_ref[...] = normed
    q_ref[...] = project(normed, weight_halves(place_ref, 0, pieces)).astype(BF16)
    k_ref[...] = project(normed, weight_halves(place_ref, 1, pieces)).astype(BF16)
    first = low_lanes(tok, size)
    for pair in range(heads // 2):
        lanes = slice(pair * 2 * size, (pair + 1) * 2 * size)
        queries, keys = q_ref[:, lanes], k_ref[:, lanes]
        for part in range(2):
            head = 2 * pair + part
            picked = jnp.where(first if part == 0 else ~first, queries, jnp.zeros_like(queries))
            scores = mm_nt(picked, keys) + bias_ref[head]
            exponent = jnp.exp(scores - jnp.max(scores, axis=-1, keepdims=True))
            probs = exponent / jnp.sum(exponent, axis=-1, keepdims=True)
            probs_ref[head] = probs.astype(BF16)


def attend_kernel(
    experts,
    place_ref,
    tokens_ref,
    normed_ref,
    gain_ref,
    router_ref,
    routes_ref,
    *refs,
):
    pieces = refs[:4]
    probs_ref, v_ref, attended_ref, residual_ref, normed_two_ref, gate_ref = refs[4:]
    heads, tok, _ = probs_ref.shape
    size = tokens_ref.shape[1] // heads
    v_ref[...] = project(normed_ref[...], weight_halves(place_ref, 0, pieces)).astype(BF16)
    first = low_lanes(tok, size)
    for pair in range(heads // 2):
        lanes = slice(pair * 2 * size, (pair + 1) * 2 * size)
        made = [mm(probs_ref[2 * pair + part], v_ref[:, lanes]) for part in range(2)]
        attended_ref[:, lanes] = jnp.where(first, made[0], made[1]).astype(BF16)
    halves = weight_halves(place_ref, 1, pieces)
    residual = tokens_ref[...].astype(F32) + project(attended_ref[...], halves)
    residual_ref[...] = residual
    factor = lax.rsqrt(jnp.mean(residual * residual, axis=-1, keepdims=True) + EPSILON)
    normed = (residual * factor * gain_ref[...]).astype(BF16)
    normed_two_ref[...] = normed
    probs = router_softmax(normed, router_ref[...], experts)
    lane = lax.broadcasted_iota(jnp.int32, probs.shape, 1)
    gate_ref[...] = jnp.sum(jnp.where(lane == routes_ref[...], probs, 0.0), axis=-1, keepdims=True)


def router_softmax(normed, router, experts):
    logits = mm(normed, router)
    lane = lax.broadcasted_iota(jnp.int32, logits.shape, 1)
    logits = jnp.where(lane < experts, logits, -1e30)
    exponent = jnp.exp(logits - jnp.max(logits, axis=-1, keepdims=True))
    return exponent / jnp.sum(exponent, axis=-1, keepdims=True)


def expert_kernel(
    experts,
    me_ref,
    rows_ref,
    cot_ref,
    router_ref,
    first_ref,
    second_ref,
    back_ref,
    hidden_ref,
    grad_pre_ref,
    produced_ref,
    grad_rows_ref,
    rows_turned_ref,
    cot_turned_ref,
    grad_logits_ref,
    made_ref,
    grad_ref,
    probs_ref,
):
    step, steps = pl.program_id(0), pl.num_programs(0)

    @pl.when(step == 0)
    def _():
        probs_ref[...] = router_softmax(rows_ref[...], router_ref[...], experts)
        rows_turned_ref[...] = rows_ref[...].T

    probs = probs_ref[...]
    chosen = lax.broadcasted_iota(jnp.int32, probs.shape, 1) == me_ref[0]
    gate = jnp.sum(jnp.where(chosen, probs, 0.0), axis=-1, keepdims=True)
    pre_act = mm(rows_ref[...], first_ref[0])
    cdf = 0.5 + 0.5 * lax.erf(pre_act * INV_ROOT_TWO)
    hidden = (pre_act * cdf).astype(BF16)
    slope = cdf + pre_act * jnp.exp(-0.5 * pre_act * pre_act) * INV_ROOT_TWO_PI
    grad_pre = (back_ref[...].astype(F32) * gate * slope).astype(BF16)
    hidden_ref[...] = hidden
    grad_pre_ref[...] = grad_pre
    made = mm(hidden, second_ref[0])
    grad = mm_nt(grad_pre, first_ref[0])

    @pl.when(step == 0)
    def _():
        made_ref[...] = made
        grad_ref[...] = grad

    @pl.when(step > 0)
    def _():
        made_ref[...] += made
        grad_ref[...] += grad

    @pl.when(step == steps - 1)
    def _():
        produced = made_ref[...].astype(BF16)
        produced_ref[...] = produced
        cot = cot_ref[...].astype(F32)
        grad_gate = jnp.sum(cot * produced.astype(F32), axis=-1, keepdims=True)
        grad_logits = (grad_gate * gate * (chosen.astype(F32) - probs)).astype(BF16)
        grad_logits_ref[...] = grad_logits
        grad_rows_ref[...] = (grad_ref[...] + mm_nt(grad_logits, router_ref[...])).astype(BF16)
        cot_turned_ref[...] = (cot * gate).astype(BF16).T


def run_expert(experts, me, rows, cot, router, w_in, w_out, slot_back, part):
    count, width = rows.shape
    inner = w_in.shape[2]
    tile = 1536
    lanes = router.shape[1]
    const = lambda shape: pl.BlockSpec(shape, lambda j, s: (0, 0))
    wide = pl.BlockSpec((count, tile), lambda j, s: (0, j))
    return pl.pallas_call(
        functools.partial(expert_kernel, experts),
        out_shape=[
            jax.ShapeDtypeStruct((count, inner), BF16),
            jax.ShapeDtypeStruct((count, inner), BF16),
            jax.ShapeDtypeStruct((count, width), BF16),
            jax.ShapeDtypeStruct((count, width), BF16),
            jax.ShapeDtypeStruct((width, count), BF16),
            jax.ShapeDtypeStruct((width, count), BF16),
            jax.ShapeDtypeStruct((count, lanes), BF16),
        ],
        grid_spec=pltpu.PrefetchScalarGridSpec(
            num_scalar_prefetch=1,
            grid=(inner // tile,),
            in_specs=[
                const((count, width)),
                const((count, width)),
                const((width, lanes)),
                pl.BlockSpec((1, width, tile), lambda j, s: (0, 0, j)),
                pl.BlockSpec((1, tile, width), lambda j, s: (0, j, 0)),
                pl.BlockSpec((count, tile), lambda j, s: (part, j)),
            ],
            out_specs=[wide, wide]
            + [const((count, width))] * 2
            + [const((width, count))] * 2
            + [const((count, lanes))],
            scratch_shapes=[
                pltpu.VMEM((count, width), F32),
                pltpu.VMEM((count, width), F32),
                pltpu.VMEM((count, lanes), F32),
            ],
        ),
        cost_estimate=estimate(9),
        compiler_params=pltpu.CompilerParams(vmem_limit_bytes=EXPERT_VMEM),
    )(me, rows, cot, router, w_in, w_out, slot_back)


def outer_kernel(place_ref, *refs):
    cots, hidden, rows, grad_pre = refs[0:2], refs[2:4], refs[4:6], refs[6:8]
    second_send, second_own, first_send, first_own = refs[8:]
    high, low, dp = place_ref[0], place_ref[1], place_ref[2]
    blocks, _, columns = second_send.shape
    for block in range(blocks):
        for core, out in ((1 - low, second_send), (low, second_own)):
            start = (2 * lax.rem(block + dp, blocks) + core) * columns
            lanes = pl.ds(pl.multiple_of(start, 128), columns)
            out[block] = (mm(cots[0][...], hidden[0][:, lanes]) + mm(cots[1][...], hidden[1][:, lanes])).astype(BF16)
    columns = first_send.shape[2]
    for index, x in enumerate((1 - high, high)):
        for core, out in ((1 - low, first_send), (low, first_own)):
            lanes = pl.ds(pl.multiple_of((2 * x + core) * columns, 128), columns)
            out[index] = (mm(rows[0][...], grad_pre[0][:, lanes]) + mm(rows[1][...], grad_pre[1][:, lanes])).astype(BF16)


def core_sum_kernel(place_ref, second_own, second_got, first_own, first_got, *outs):
    high, dp = place_ref[0], place_ref[2]
    blocks, width, _ = second_own.shape
    half, rows = width // 2, width // 4
    for block in range(blocks):
        total = (second_own[block].astype(F32) + second_got[block].astype(F32)).astype(BF16)
        send = jnp.where(high == 0, total[half:], total[:half])
        kept = jnp.where(high == 0, total[:half], total[half:])
        outs[block][0] = send[:rows]
        outs[block][1] = kept[:rows]
        at = lax.rem(block + dp, blocks)
        outs[blocks][at] = send[rows:]
        outs[blocks + 1][at] = kept[rows:]
    rows = width // blocks
    for index in range(2):
        for block in range(blocks):
            lines = slice(block * rows, (block + 1) * rows)
            total = first_own[index, lines].astype(F32) + first_got[index, lines].astype(F32)
            outs[blocks + 2 + index][lax.rem(block - dp + blocks, blocks)] = total.astype(BF16)


def add_kernel(count, *refs):
    ins, outs = refs[: len(refs) - count], refs[len(refs) - count :]
    for index, out in enumerate(outs):
        total = 0.0
        for ref in ins:
            total = total + (ref[index] if count > 1 else ref[...]).astype(F32)
        out[...] = total.astype(BF16)


def add_arrays(arrays, count=1, us=BIG):
    shape = arrays[0].shape[1:] if count > 1 else arrays[0].shape
    outs = whole_call(functools.partial(add_kernel, count), [(shape, BF16)] * count, [], arrays, us=us)
    return outs if count > 1 else outs[0]


def core_add_kernel(place_ref, keep_ref, got_ref, send_ref, mine_ref):
    blocks, rows = send_ref.shape[1], send_ref.shape[2]
    me = place_ref[3]
    for matrix in range(2):
        for block in range(blocks):
            start = 2 * block * rows
            total = keep_ref[matrix, start : start + 2 * rows].astype(F32)
            total = (total + got_ref[matrix, start : start + 2 * rows].astype(F32)).astype(BF16)
            one, two = total[:rows], total[rows:]
            mine_ref[matrix, block] = jnp.where(me == 0, one, two)
            send_ref[matrix, block] = jnp.where(me == 0, two, one)


def pair_add_kernel(place_ref, keep_ref, got_ref, small_keep_ref, small_got_ref, send_ref, mine_ref):
    high = place_ref[0]
    rows = keep_ref.shape[2]
    send_ref[:, :rows] = (keep_ref[1 - high].astype(F32) + got_ref[1 - high].astype(F32)).astype(BF16)
    mine_ref[:, :rows] = (keep_ref[high].astype(F32) + got_ref[high].astype(F32)).astype(BF16)
    small = (small_keep_ref[...].astype(F32) + small_got_ref[...].astype(F32)).astype(BF16)
    send_ref[:, rows:] = small
    mine_ref[:, rows:] = small


def plain_add_kernel(one, two, out):
    out[...] = (one[...].astype(F32) + two[...].astype(F32)).astype(BF16)


def sum_kernel(blocks, out):
    total = blocks[0].astype(F32)
    for block in range(1, blocks.shape[0]):
        total = total + blocks[block].astype(F32)
    out[...] = total.astype(BF16)


def second_sum_kernel(early_keep, early_got, blocks, out):
    low = blocks[0].astype(F32)
    for block in range(1, blocks.shape[0]):
        low = low + blocks[block].astype(F32)
    high = early_keep[1].astype(F32) + early_got[...].astype(F32)
    out[...] = jnp.concatenate([high, low], axis=0).T.astype(BF16)


def lay_rows_kernel(rows, place_ref, own_ref, got_ref, out_ref, *rest):
    blocks = own_ref.shape[0]
    me = place_ref[3]
    for block in range(blocks):
        at = lax.rem(place_ref[2] - block + blocks, blocks)
        own, got = own_ref[at], got_ref[at]
        both = (jnp.where(me == 0, own, got), jnp.where(me == 0, got, own))
        for index in range(2):
            start = (2 * block + index) * rows
            out_ref[start : start + rows, :] = both[index][:rows]
            for ref in rest:
                ref[2 * block + index] = both[index][rows:, : ref.shape[2]]


def attend_back_kernel(
    place_ref,
    mask_ref,
    own_ref,
    got_ref,
    residual_ref,
    cot_ref,
    gain_ref,
    attended_ref,
    *refs,
):
    pieces = refs[:4]
    q_ref, k_ref, v_ref, probs_ref, normed_ref, keep_ref, ds_ref, gq_ref, gk_ref, gv_ref = refs[4:14]
    grad_res_ref, gain_grad_ref, send_ref, ga_ref, gat_ref, qt_ref, kt_ref = refs[14:]
    heads, tok, _ = probs_ref.shape
    size = residual_ref.shape[1] // heads
    low = place_ref[1]

    def store(index, grad):
        grad = grad.astype(BF16)

        @pl.when(low == index % 2)
        def _():
            keep_ref[index // 2] = grad

        @pl.when(low != index % 2)
        def _():
            send_ref[index // 2] = grad

    grad_two = jnp.where(mask_ref[...] > 0, own_ref[...], got_ref[...]).astype(F32)
    residual = residual_ref[...]
    factor = lax.rsqrt(jnp.mean(residual * residual, axis=-1, keepdims=True) + EPSILON)
    scaled = grad_two * gain_ref[...]
    inner = jnp.mean(scaled * residual, axis=-1, keepdims=True)
    grad_res = cot_ref[...].astype(F32) + factor * scaled - residual * (factor * factor * factor) * inner
    grad_res_ref[...] = grad_res
    gain_grad_ref[...] = jnp.sum(grad_two * residual * factor, axis=0, keepdims=True)
    grad_attn = grad_res.astype(BF16)
    store(3, mm(attended_ref[...].T, grad_attn))
    left, right = weight_halves(place_ref, 1, pieces)
    half = left.shape[1]
    ga_ref[...] = (mm_nt(grad_attn[:, :half], left) + mm_nt(grad_attn[:, half:], right)).astype(BF16)
    gat_ref[...] = (mm_nt(left, grad_attn[:, :half]) + mm_nt(right, grad_attn[:, half:])).astype(BF16)
    qt_ref[...] = q_ref[...].T
    kt_ref[...] = k_ref[...].T
    first = low_lanes(tok, size)
    for head in range(heads):
        lanes = slice(head // 2 * 2 * size, (head // 2 + 1) * 2 * size)
        rows = slice(head * size, (head + 1) * size)
        grads = ga_ref[:, lanes]
        picked = jnp.where(first if head % 2 == 0 else ~first, grads, jnp.zeros_like(grads))
        grad_probs = mm_nt(picked, v_ref[:, lanes])
        probs = probs_ref[head]
        wide = probs.astype(F32)
        total = jnp.sum(wide * grad_probs, axis=-1, keepdims=True)
        ds = (wide * (grad_probs - total)).astype(BF16)
        ds_ref[head] = ds
        gq_ref[rows, :] = mm_nt(kt_ref[rows, :], ds).astype(BF16)
        gk_ref[rows, :] = mm(qt_ref[rows, :], ds).astype(BF16)
        gv_ref[rows, :] = mm(gat_ref[rows, :], probs).astype(BF16)
    turned = normed_ref[...].T
    store(0, mm_nt(turned, gq_ref[...]))
    store(1, mm_nt(turned, gk_ref[...]))
    store(2, mm_nt(turned, gv_ref[...]))


def finish_kernel(
    place_ref,
    tokens_ref,
    gain_ref,
    *refs,
):
    qk_pieces, vo_pieces = refs[:4], refs[4:8]
    gq_ref, gk_ref, gv_ref, ds_ref, grad_res_ref, gain_two_ref, onehot_ref = refs[8:15]
    turn_a_ref, turn_b_ref, logits_a_ref, logits_b_ref, grad_tokens_ref, small_ref = refs[15:]
    heads, tok, _ = ds_ref.shape
    window, lanes = onehot_ref.shape
    grad = project_back(gq_ref[...], weight_halves(place_ref, 0, qk_pieces))
    grad = grad + project_back(gk_ref[...], weight_halves(place_ref, 1, qk_pieces))
    grad = grad + project_back(gv_ref[...], weight_halves(place_ref, 0, vo_pieces))
    grad = grad.T
    values = tokens_ref[...].astype(F32)
    factor = lax.rsqrt(jnp.mean(values * values, axis=-1, keepdims=True) + EPSILON)
    scaled = grad * gain_ref[...]
    inner = jnp.mean(scaled * values, axis=-1, keepdims=True)
    grad_tokens_ref[...] = grad_res_ref[...] + factor * scaled - values * (factor * factor * factor) * inner
    experts = small_ref.shape[0] - 2 - heads
    small_ref[0:1, :] = jnp.sum(grad * values * factor, axis=0, keepdims=True)
    small_ref[1:2, :] = gain_two_ref[...]
    router = mm(turn_a_ref[...], logits_a_ref[...]) + mm(turn_b_ref[...], logits_b_ref[...])
    small_ref[2 : 2 + experts, :] = router.T[:experts]
    small_ref[2 + experts :, :] = jnp.zeros((heads, small_ref.shape[1]), F32)
    row = lax.broadcasted_iota(jnp.int32, (tok, tok), 0)
    column = lax.broadcasted_iota(jnp.int32, (tok, tok), 1)
    turned = (row + column == tok - 1).astype(BF16)
    for head in range(heads):
        flipped = mm(turned, ds_ref[head])
        wide = jnp.concatenate([flipped, jnp.zeros((tok, window - tok), F32)], axis=1)
        rolled = pltpu.roll(wide, window - tok + 1, 1, stride=1, stride_axis=0)
        diagonal = jnp.broadcast_to(jnp.sum(rolled, axis=0, keepdims=True), (8, window))
        table = jnp.dot(diagonal, onehot_ref[...], precision=lax.Precision.HIGHEST, preferred_element_type=F32)
        small_ref[2 + experts + head : 3 + experts + head, 0:lanes] = table[0:1]


def second_shared_kernel(place_ref, *refs):
    pieces, out = refs[:4], refs[4]
    rows, columns = pieces[0].shape
    for target in range(4):
        x, core = target // 2, target % 2
        out[0, core * rows : (core + 1) * rows, x * columns : (x + 1) * columns] = choose(place_ref, target, pieces).astype(F32)


def first_shared_kernel(place_ref, *refs):
    pieces, out = refs[:4], refs[4]
    columns = pieces[0].shape[1]
    for target in range(4):
        out[0, :, target * columns : (target + 1) * columns] = choose(place_ref, target, pieces).astype(F32)


def attention_shared_kernel(place_ref, *refs):
    for target in range(4):
        refs[4 + target][...] = choose(place_ref, target, refs[:4]).astype(F32)


def spread(values, *others):
    far = rep_swap(values, 2)
    if others:
        far = after(far, *others)
    return [values, rep_swap(values, 1), far, rep_swap(far, 1)]


def after(values, *others):
    return lax.optimization_barrier((values,) + others)[0]


def local(
    tokens,
    doc_ids,
    routes,
    cotangent,
    attn_gain,
    w_query,
    w_key,
    w_value,
    w_output,
    rel_table,
    ffn_gain,
    w_router,
    w_in,
    w_out,
):
    tok_rows, width = tokens.shape
    head_count = rel_table.shape[1]
    experts = w_router.shape[1]
    dp_count = lax.axis_size("dp")
    expert_axis = lax.axis_size("expert")
    capacity = 2 * tok_rows // expert_axis
    inner = w_in.shape[2]
    rep = lax.axis_index("rep")
    high, low = rep // 2, rep % 2
    me = lax.axis_index("expert")
    dp = lax.axis_index("dp")
    place = jnp.stack([high, low, dp, me]).astype(jnp.int32)
    shard_rows = w_query.shape[0]
    lanes = 128
    slots = experts * capacity

    onehot = bucket_onehot(tok_rows, rel_table.shape[0])
    diag_values = jnp.dot(onehot, rel_table, precision=lax.Precision.HIGHEST).T
    square = (head_count, tok_rows, tok_rows)
    (bias,) = whole_call(
        bias_kernel, [(square, F32)], [], [diag_values, doc_ids[None, :], doc_ids[:, None]], us=2
    )

    half = width // 2
    small = jnp.concatenate([attn_gain[None], ffn_gain[None], w_router.T], axis=0)
    small_rows = -(-(2 + experts) // 16) * 16
    small = jnp.pad(small, ((0, small_rows - 2 - experts), (0, half - shard_rows)))

    def quarter(one, two):
        return lax.dynamic_slice_in_dim(jnp.where(high == 0, one, two), low * half, half, 1)

    qk_quarter = jnp.concatenate([quarter(w_query, w_key), small], axis=0)
    vo_quarter = quarter(w_value, w_output)
    if expert_axis == 2:

        def along_dp(values):
            return jnp.stack([values] + [shift(values, "dp", step) for step in range(1, dp_count)])

        qk_own, vo_own = along_dp(qk_quarter), along_dp(vo_quarter)
        qk_own = after(qk_own, bias)
        qk_got = shift(qk_own, "expert", 1)
        vo_got = shift(vo_own, "expert", 1)
        rest_shape = (dp_count * expert_axis, small_rows, lanes)
        qk_mine, rest = whole_call(
            functools.partial(lay_rows_kernel, shard_rows),
            [((width, half), BF16), (rest_shape, BF16)],
            [place],
            [qk_own, qk_got],
            us=1,
        )
        (vo_mine,) = whole_call(
            functools.partial(lay_rows_kernel, shard_rows), [((width, half), BF16)], [place], [vo_own, vo_got], us=1
        )
    else:
        rows_all = lax.all_gather(qk_quarter, ("dp", "expert"), axis=0)
        qk_mine, rest = rows_all[:, :shard_rows].reshape(width, half), rows_all[:, shard_rows:]
        vo_mine = lax.all_gather(vo_quarter, ("dp", "expert"), axis=0, tiled=True)
    rest = jnp.moveaxis(rest[:, : 2 + experts, :shard_rows], 1, 0).reshape(2 + experts, width)
    gain_one = rest[0:1].astype(F32)
    gain_two = rest[1:2].astype(F32)
    router = jnp.pad(rest[2:].T, ((0, 0), (0, lanes - experts)))
    qk_pieces = spread(qk_mine)

    route_ids = routes[:, 0]
    direct = expert_axis == 2 and capacity == tok_rows
    if direct:
        own_mask = (routes == me).astype(F32)

        def send(values):
            return values, shift(values, "expert", 1)

        def back(one, two):
            return one, shift(two, "expert", 1)

        zero = jnp.zeros_like(cotangent)
        cot_a = jnp.where(routes == me, cotangent, zero)
        cot_b = shift(after(jnp.where(routes == me, zero, cotangent), vo_got), "expert", 1)
    else:
        own_mask = jnp.ones((tok_rows, 1), F32)
        chosen = (route_ids[:, None] == jnp.arange(experts, dtype=jnp.int32)[None, :]).astype(jnp.int32)
        slot_rank = jnp.sum(jnp.cumsum(chosen, axis=0) * chosen, axis=-1) - 1
        slot_index = route_ids * capacity + slot_rank
        place_of = (jnp.arange(slots, dtype=jnp.int32)[:, None] == slot_index[None, :]).astype(BF16)

        def send(values):
            filled = mm(place_of, values).astype(BF16)
            filled = lax.all_to_all(filled, "expert", split_axis=0, concat_axis=0, tiled=True)
            return filled[: slots // 2], filled[slots // 2 :]

        def back(one, two):
            rows = jnp.concatenate([one, two], axis=0)
            rows = lax.all_to_all(rows, "expert", split_axis=0, concat_axis=0, tiled=True)
            rows = mm_tn(place_of, rows).astype(BF16)
            return rows, rows

        cot_a, cot_b = send(cotangent)

    slot_cot = jnp.concatenate([cot_a, cot_b], axis=0)
    slot_back = mm_nt(slot_cot, w_out[0]).astype(BF16)

    flat = (tok_rows, width)
    normed_one, queries, keys, probs = whole_call(
        scores_kernel,
        [(flat, BF16)] * 3 + [(square, BF16)],
        [place],
        [tokens, gain_one, *qk_pieces, bias],
        us=4,
    )
    vo_pieces = spread(after(vo_mine, qk_pieces[2]), slot_back, normed_one)
    values, attended, residual, normed_two, gate = whole_call(
        functools.partial(attend_kernel, experts),
        [(flat, BF16), (flat, BF16), (flat, F32), (flat, BF16), ((tok_rows, 1), F32)],
        [place],
        [tokens, normed_one, gain_two, router, routes, *vo_pieces, probs],
        us=4,
    )

    rows_a, rows_b = send(normed_two)
    where_me = me[None].astype(jnp.int32)
    run = functools.partial(run_expert, experts, where_me)
    hid_a, pre_a, made_a, grad_a, turn_a, cot_turn_a, logits_a = run(
        rows_a, cot_a, router, w_in, w_out, slot_back, 0
    )
    hid_b, pre_b, made_b, grad_b, turn_b, cot_turn_b, logits_b = run(
        rows_b, cot_b, router, w_in, w_out, slot_back, 1
    )
    grad_own, grad_got = back(grad_a, grad_b)

    quarter_columns = inner // 4
    second_shape, first_shape = (dp_count, width, width // 2), (2, width, quarter_columns)
    second_send, second_own, first_send, first_own = whole_call(
        outer_kernel,
        [(second_shape, BF16)] * 2 + [(first_shape, BF16)] * 2,
        [place],
        [cot_turn_a, cot_turn_b, hid_a, hid_b, turn_a, turn_b, pre_a, pre_b],
        us=BIG,
    )
    second_in = rep_swap(after(second_send, grad_got), 1)
    first_in = rep_swap(after(first_send, grad_got), 1)

    keep_part, grad_scores, grad_q, grad_k, grad_v, grad_res, grad_gain_two, send_part = whole_call(
        attend_back_kernel,
        [((2, width, width), BF16), (square, BF16)]
        + [((width, tok_rows), BF16)] * 3
        + [(flat, F32), ((1, width), F32)]
        + [((2, width, width), BF16)],
        [place],
        [own_mask, grad_own, grad_got, residual, cotangent, gain_two, attended]
        + [*vo_pieces, queries, keys, values, probs, normed_one],
        scratch=[pltpu.VMEM(flat, BF16)] + [pltpu.VMEM((width, tok_rows), BF16)] * 3,
        us=0,
    )
    core_got = rep_swap(send_part, 1)

    *early, second_send, second_keep, first_send, first_keep = whole_call(
        core_sum_kernel,
        [((2, width // 4, width // 2), BF16)] * dp_count
        + [((dp_count, width // 4, width // 2), BF16)] * 2
        + [((dp_count, width // dp_count, quarter_columns), BF16)] * 2,
        [place],
        [after(second_own, grad_res), second_in, first_own, first_in],
        us=0,
    )

    def z_sent(blocks):
        return [blocks[0]] + [shift(blocks[step], "dp", step) for step in range(1, dp_count)]

    second_got = rep_swap(second_send, 2)
    first_got = rep_swap(after(first_send, second_got), 2)
    early_z = z_sent(early)

    if expert_axis == 2:
        cross = (2, dp_count, shard_rows, width)
        y_send, y_keep = whole_call(
            core_add_kernel, [(cross, BF16)] * 2, [place], [after(keep_part, early[0]), core_got], us=BIG
        )
        y_got = shift(y_send, "expert", 1)
        token = y_send
    else:
        part = add_pair(after(keep_part, early[0]), core_got)
        part = part.reshape(2, dp_count, expert_axis, shard_rows, width)
        part = sum_over(part, "expert", 2)
        token = part

    wide_onehot = jnp.pad(onehot, ((0, 0), (0, lanes - onehot.shape[1])))
    grad_tokens, small = whole_call(
        finish_kernel,
        [(flat, F32), ((2 + experts + head_count, width), F32)],
        [place],
        [tokens, gain_one, *qk_pieces, *vo_pieces, grad_q, grad_k, grad_v, grad_scores]
        + [after(grad_res, token), grad_gain_two, wide_onehot, turn_a, turn_b, logits_a, logits_b],
        us=BIG,
    )
    (second_blocks,) = whole_call(
        plain_add_kernel, [(second_keep.shape, BF16)], [], [after(second_keep, grad_tokens), second_got], us=0
    )
    early_sum = add_arrays([after(early_z[0], second_blocks)] + early_z[1:], us=0)
    early_got = rep_swap(early_sum[0], 2)
    second_z = lax.all_to_all(after(second_blocks, early_sum), "dp", split_axis=0, concat_axis=0, tiled=True)
    if expert_axis == 2:
        shards = dp_count * expert_axis
        count = 2 + experts
        small_rows = -(-(count + head_count) // 16) * 16
        split = jnp.swapaxes(small[:count].reshape(count, shards, shard_rows), 0, 1).astype(BF16)
        split = jnp.pad(split, ((0, 0), (0, 0), (0, width - shard_rows)))
        table = jnp.broadcast_to(small[count:].astype(BF16)[None], (shards, head_count, width))
        small = jnp.concatenate([split, table], axis=1)
        small = jnp.pad(small, ((0, 0), (0, small_rows - count - head_count), (0, 0)))
        small = after(small, early_sum)
        small = add_pair(small, rep_swap(small, 1)).reshape(dp_count, 2, small_rows, width)
        small_got = shift(pick(small, 1 - me, 1), "expert", 1)
        small_keep = pick(small, me, 1)
    first_z = z_sent(add_arrays([after(first_keep, early_sum), first_got], dp_count, us=0))
    if expert_axis == 2:
        x_send, x_keep = whole_call(
            pair_add_kernel,
            [((dp_count, shard_rows + small_rows, width), BF16)] * 2,
            [place],
            [after(y_keep, first_z[0]), y_got, small_keep, small_got],
            us=0,
        )
        x_got = rep_swap(x_send, 2)
        token = x_keep
    else:
        x_part = add_pair(pick(part, high, 0), rep_swap(pick(part, 1 - high, 0), 2))
        token = x_part
    half_rows, half_columns = second_z.shape[1:]
    (second_sum,) = whole_call(
        second_sum_kernel,
        [((half_columns, 2 * half_rows), BF16)],
        [],
        [after(early_sum, token), early_got, second_z],
        us=0,
    )
    second_pieces = spread(second_sum)
    if expert_axis == 2:
        (x_sum,) = whole_call(
            plain_add_kernel, [(x_keep.shape, BF16)], [], [after(x_keep, second_sum), x_got], us=0
        )
        attn_z = lax.all_to_all(x_sum, "dp", split_axis=0, concat_axis=0, tiled=True)
        token = x_sum
    made_own, made_got = back(made_a, after(made_b, token))
    (grad_w_out,) = whole_call(
        second_shared_kernel, [((1, inner // dp_count, width), F32)], [place], second_pieces
    )
    first_sum = add_arrays([after(first_z[0], token)] + first_z[1:], us=0)
    first_pieces = spread(first_sum)
    if expert_axis == 2:
        (attn_sum,) = whole_call(
            sum_kernel, [(x_keep.shape[1:], BF16)], [], [after(attn_z, first_sum)], us=0
        )
        attn_pieces = spread(attn_sum[:shard_rows])
        small = attn_sum[shard_rows:].astype(F32)
        table_total = small[2 + experts : 2 + experts + head_count, : rel_table.shape[0]].T
        small = small[: 2 + experts, :shard_rows]
    else:
        attn_pieces = spread(sum_over(x_part, "dp", 0))
        small = lax.psum(small, ("rep", "dp", "expert"))
        table_total = small[2 + experts :, : rel_table.shape[0]].T
        row_start = (dp * expert_axis + me) * shard_rows
        small = lax.dynamic_slice_in_dim(small[: 2 + experts], row_start, shard_rows, 1)
    (grad_w_in,) = whole_call(first_shared_kernel, [((1, width // dp_count, inner), F32)], [place], first_pieces)
    owned = whole_call(attention_shared_kernel, [((shard_rows, width), F32)] * 4, [place], attn_pieces)

    expert_rows = jnp.where(own_mask > 0, made_own, made_got).astype(F32)
    mixed = (residual + gate * expert_rows).astype(BF16)
    return (
        mixed,
        grad_tokens,
        small[0],
        owned[0],
        owned[1],
        owned[2],
        owned[3],
        table_total,
        small[1],
        small[2:].T,
        grad_w_in,
        grad_w_out,
    )


def solution(mesh):
    rows = P(("rep", "dp", "expert"), None)
    split = P(("dp", "expert"), None)
    vector = P(("dp", "expert"))
    return jax.shard_map(
        local,
        mesh=mesh,
        in_specs=(
            rows,
            P(("rep", "dp", "expert")),
            rows,
            rows,
            vector,
            split,
            split,
            split,
            split,
            P(),
            vector,
            split,
            P("expert", None, None),
            P("expert", None, None),
        ),
        out_specs=(
            rows,
            rows,
            vector,
            split,
            split,
            split,
            split,
            P(),
            vector,
            split,
            P("expert", "dp", None),
            P("expert", "dp", None),
        ),
        check_vma=False,
    )
```
